256 devices in a mesh: group: 8 (over z), member: 32 (over y, x, core).
Axes of the slice: x: 4, y: 4, z: 8, core: 2. Of those that a mesh axis runs over, the one named last changes fastest.
Arguments:
- patterns: float32 [256, 2, 256, 512], P('group', None, 'member'), may hold values from -6 to 6
- operators: float32 [100, 2, 256, 512], P(None, None, 'member'), may hold values from -1 to 1
- partners: int32 [256, 8], P('group'), may hold values from 0 to 255, as said below
- operator_index: int32 [256, 8], P('group'), may hold values from 0 to 99
- child_parent: int32 [512], P('group'), may hold values from 0 to 255, as said below
- child_octant: int32 [512], P('group'), may hold values from 0 to 7, as said below
Outputs:
- child_patterns: float32 [512, 2, 128, 256], P('group', None, 'member')
The draws below stay inside these ranges and needn't reach their ends.
Inputs may be any that keep to these rules, and one draw needn't show every extreme that they name: `partners`: an entry of cluster c's list lies in c's own group block (clusters g * 32 to (g + 1) * 32 - 1); only the first 8 clusters of a block may also name any of the last 8 clusters of the previous block, and only the last 8 clusters any of the first 8 clusters of the next block. `child_parent`: the parent of a child in child block g (children g * 64 to (g + 1) * 64 - 1) lies in cluster block g; every cluster has at least one child; every cluster has 1 to 3 children, and in every block some cluster has exactly 3. `child_octant`: children of one parent have different octants.
All inputs are finite; a program needn't handle non-finite values.
Results may differ from the reference program's by a relative error of at most 0.0003.
Values sent between devices are 32-bit elements; how exact they have to be, the bound alone decides.
A program may use at most 64 MiB of HBM per device.

```python
import math
import jax
import jax.numpy as jnp
from jax import lax

NT = 256
NP = 512
NTC = 128
NPC = 256
NOPS = 100
NPART = 8
PAR_DEV = 1
CL_GRP = 32
CLUSTERS = 256
BAND = 8
CH_GRP = 64
CHILDREN = 512


def children_helper(key):
    groups = CLUSTERS // CL_GRP
    members = CL_GRP // PAR_DEV
    key_a, key_b, key_c = jax.random.split(jax.random.fold_in(key, 71), 3)
    swing = jax.random.randint(key_a, (groups, members // 2), -PAR_DEV, PAR_DEV + 1)
    forced = jax.random.randint(key_b, (groups, 1), 0, members // 2)
    swing = jnp.where(jnp.arange(members // 2)[None, :] == forced, PAR_DEV, swing)
    counts = jnp.stack([2 * PAR_DEV + swing, 2 * PAR_DEV - swing], axis=2).reshape(groups, members)
    run_ends = jnp.cumsum(counts, axis=1)
    starts = run_ends - counts
    slot_ids = jnp.arange(CH_GRP)
    holder = jnp.sum((slot_ids[None, :, None] >= run_ends[:, None, :]).astype(jnp.int32), axis=2)
    offset = slot_ids[None, :] - jnp.take_along_axis(starts, holder, axis=1)
    perm_keys = jax.random.split(key_c, groups * members)

    def one_perm(single_key):
        return jax.random.permutation(single_key, 8)
    octant_perms = jax.vmap(one_perm)(perm_keys).reshape(groups, members * 8)
    octant_ids = jnp.take_along_axis(octant_perms, holder * 8 + offset // PAR_DEV, axis=1)
    parent_ids = jnp.arange(groups)[:, None] * CL_GRP + holder * PAR_DEV + offset % PAR_DEV
    return (parent_ids.reshape(-1).astype(jnp.int32), octant_ids.reshape(-1).astype(jnp.int32))


def draw_child_parent(key, part):
    return children_helper(key)[0]


def draw_child_octant(key, part):
    return children_helper(key)[1]


def draw_partners(key, part):
    groups = CLUSTERS // CL_GRP
    key_a, key_b, key_c = jax.random.split(jax.random.fold_in(key, 13), 3)
    cluster_ids = jnp.arange(CLUSTERS)[:, None]
    group_ids = cluster_ids // CL_GRP
    local_ids = cluster_ids % CL_GRP
    same_block = group_ids * CL_GRP + jax.random.randint(key_a, (CLUSTERS, NPART), 0, CL_GRP)
    cross_pick = jax.random.randint(key_b, (CLUSTERS, NPART), 0, 3)
    edge_ids = jax.random.randint(key_c, (CLUSTERS, NPART), 0, BAND)
    from_below = group_ids * CL_GRP - BAND + edge_ids
    from_above = (group_ids + 1) * CL_GRP + edge_ids
    use_below = (local_ids < BAND) & (group_ids > 0) & (cross_pick == 0)
    use_above = (local_ids >= CL_GRP - BAND) & (group_ids < groups - 1) & (cross_pick == 1)
    return jnp.where(use_below, from_below, jnp.where(use_above, from_above, same_block)).astype(jnp.int32)


def plant(values, rng, least, largest):
    place = [jax.random.randint(jax.random.fold_in(rng, axis), (), 0, length) for axis, length in enumerate(values.shape)]
    longest = values.shape.index(max(values.shape))
    neighbour = place[:longest] + [(place[longest] + 1) % values.shape[longest]] + place[longest + 1:]
    return values.at[tuple(place)].set(least).at[tuple(neighbour)].set(largest)


def block_levels(own_key, shape, pieces, smallest, high):
    loudness, own = 1.0, jax.random.fold_in(own_key, 6)
    for position, shards_of in pieces:
        heights = jnp.exp(jax.random.uniform(jax.random.fold_in(own, position), (shards_of,), jnp.float32, smallest / len(pieces), high / len(pieces)))
        loudness = loudness * jnp.repeat(heights, shape[position] // shards_of).reshape([-1 if axis == position else 1 for axis in range(len(shape))])
    return loudness


def bell_draw(key, extent, width, reach, shards=(), kind=jnp.bfloat16):
    values = jax.random.normal(key, extent, jnp.float32) * width
    if len(shards) > 0:
        values = block_levels(key, extent, shards, -0.22, 0.18) * values
    return jnp.clip(values, min=-reach, max=reach).astype(kind)


def setup_inputs(seed: int = 0) -> dict:
    splits = jax.random.split(jax.random.key(seed), 7)
    return {
        "patterns": bell_draw(splits[0], (CLUSTERS, 2, NT, NP), 1.0, 6.0, ((0, 8), (2, 32)), jnp.float32),
        "operators": bell_draw(splits[1], (NOPS, 2, NT, NP), 0.16, 1.0, ((2, 32),), jnp.float32),
        "partners": draw_partners(jax.random.fold_in(splits[6], 71), 0),
        "operator_index": plant(jax.random.randint(splits[3], (CLUSTERS, NPART), 0, NOPS), jax.random.fold_in(splits[3], 1), 0, NOPS - 1).astype(jnp.int32),
        "child_parent": draw_child_parent(jax.random.fold_in(splits[6], 71), 0),
        "child_octant": draw_child_octant(jax.random.fold_in(splits[6], 71), 0),
    }


shift_reach = 6.0


def anterp_tables(theta_count, phi_count, theta_child, phi_child):
    theta_fine = math.pi * (jnp.arange(theta_count, dtype=jnp.float32) + 0.5) / theta_count
    theta_coarse = math.pi * (jnp.arange(theta_child, dtype=jnp.float32) + 0.5) / theta_child
    orders = jnp.arange(theta_child, dtype=jnp.float32)
    weights = jnp.where(orders > 0, 2.0, 1.0).astype(jnp.float32)
    theta_matrix = jnp.dot(jnp.cos(jnp.outer(theta_coarse, orders)) * weights, jnp.cos(jnp.outer(theta_fine, orders)).T, precision=lax.Precision.HIGHEST) / theta_count
    phi_fine = 2.0 * math.pi * jnp.arange(phi_count, dtype=jnp.float32) / phi_count
    phi_coarse = 2.0 * math.pi * jnp.arange(phi_child, dtype=jnp.float32) / phi_child
    phi_modes = jnp.arange(phi_child // 2 + 1, dtype=jnp.float32)
    mode_weights = jnp.where((phi_modes > 0) & (phi_modes < phi_child // 2), 2.0, 1.0).astype(jnp.float32)
    cos_part = jnp.dot(jnp.cos(jnp.outer(phi_coarse, phi_modes)) * mode_weights, jnp.cos(jnp.outer(phi_fine, phi_modes)).T, precision=lax.Precision.HIGHEST)
    sin_part = jnp.dot(jnp.sin(jnp.outer(phi_coarse, phi_modes)) * mode_weights, jnp.sin(jnp.outer(phi_fine, phi_modes)).T, precision=lax.Precision.HIGHEST)
    phi_matrix = (cos_part + sin_part) / phi_count
    sin_theta = jnp.sin(theta_fine)[:, None]
    dir_x = sin_theta * jnp.cos(phi_fine)[None, :]
    dir_y = sin_theta * jnp.sin(phi_fine)[None, :]
    dir_z = jnp.cos(theta_fine)[:, None] * jnp.ones((1, phi_count), jnp.float32)
    return theta_matrix, phi_matrix, dir_x, dir_y, dir_z


def anterpolate(parents, octants, tables):
    theta_matrix, phi_matrix, dir_x, dir_y, dir_z = tables
    sign_x = (1 - 2 * (octants % 2)).astype(jnp.float32)[:, None, None]
    sign_y = (1 - 2 * ((octants // 2) % 2)).astype(jnp.float32)[:, None, None]
    sign_z = (1 - 2 * (octants // 4)).astype(jnp.float32)[:, None, None]
    phase_arg = shift_reach * (sign_x * dir_x + sign_y * dir_y + sign_z * dir_z)
    cosine = jnp.cos(phase_arg)
    sine_part = jnp.sin(phase_arg)
    real_part = parents[:, 0] * cosine - parents[:, 1] * sine_part
    imag_part = parents[:, 0] * sine_part + parents[:, 1] * cosine
    shifted = jnp.stack([real_part, imag_part], axis=1)
    coarse = jnp.einsum("jt,sktf->skjf", theta_matrix, shifted, precision=lax.Precision.HIGHEST)
    return jnp.einsum("skjf,gf->skjg", coarse, phi_matrix, precision=lax.Precision.HIGHEST)


def reference(patterns, operators, partners, operator_index, child_parent, child_octant):
    def add_partner(column, running):
        partner_rows = jnp.take(patterns, partners[:, column], axis=0)
        factors = jnp.take(operators, operator_index[:, column], axis=0)
        real_part = factors[:, 0] * partner_rows[:, 0] - factors[:, 1] * partner_rows[:, 1]
        imag_part = factors[:, 0] * partner_rows[:, 1] + factors[:, 1] * partner_rows[:, 0]
        return running + jnp.stack([real_part, imag_part], axis=1)

    translated = lax.fori_loop(0, NPART, add_partner, jnp.zeros(patterns.shape, jnp.float32))
    tables = anterp_tables(NT, NP, NTC, NPC)

    def child_block(block_in):
        parent_ids, octants = block_in
        return anterpolate(jnp.take(translated, parent_ids, axis=0), octants, tables)

    blocks = lax.map(child_block, (child_parent.reshape(-1, 16), child_octant.reshape(-1, 16)))
    return blocks.reshape(CHILDREN, 2, NTC, NPC)
```

```python
import functools

import jax
import jax.numpy as jnp
import ml_dtypes
import numpy as np
from jax import lax
from jax.experimental import pallas as pl
from jax.experimental.pallas import tpu as pltpu
from jax.sharding import PartitionSpec as P

MESH = pl.DeviceIdType.MESH

NT, NP, NTC, NPC = 256, 512, 128, 256
NPART = 8
CL = 32
CH = 64
BAND = 8
MEM = 32
LAT = NT // MEM
OUT_LAT = NTC // MEM
PER = CH // MEM
REACH = 6.0


def split(values):
    high = values.astype(ml_dtypes.bfloat16)
    low = (values - high.astype(np.float64)).astype(ml_dtypes.bfloat16)
    return high, low


def tables():
    theta_fine = np.pi * (np.arange(NT) + 0.5) / NT
    theta_coarse = np.pi * (np.arange(NTC) + 0.5) / NTC
    orders = np.arange(NTC)
    weights = np.where(orders > 0, 2.0, 1.0)
    theta = (np.cos(np.outer(theta_coarse, orders)) * weights) @ np.cos(np.outer(theta_fine, orders)).T / NT
    phi_fine = 2.0 * np.pi * np.arange(NP) / NP
    phi_coarse = 2.0 * np.pi * np.arange(NPC) / NPC
    modes = np.arange(NPC // 2 + 1)
    mode_weights = np.where((modes > 0) & (modes < NPC // 2), 2.0, 1.0)
    phi = (
        (np.cos(np.outer(phi_coarse, modes)) * mode_weights) @ np.cos(np.outer(phi_fine, modes)).T
        + (np.sin(np.outer(phi_coarse, modes)) * mode_weights) @ np.sin(np.outer(phi_fine, modes)).T
    ) / NP
    big = np.zeros((MEM, 2, OUT_LAT, MEM, 2, LAT))
    blocks = theta.reshape(MEM, OUT_LAT, MEM, LAT)
    for part in range(2):
        big[:, part, :, :, part, :] = blocks
    theta_high, theta_low = split(big.reshape(MEM * 2 * OUT_LAT, MEM * 2 * LAT))
    phi_high, phi_low = split(phi.T)
    arg = REACH * np.sin(theta_fine)[:, None] * np.cos(phi_fine)[None, :]
    wave_x = np.stack([np.cos(arg), np.sin(arg)]).reshape(2, MEM, LAT, NP).swapaxes(0, 1)
    arg = np.broadcast_to(REACH * np.cos(theta_fine)[:, None], (NT, 128))
    wave_z = np.stack([np.cos(arg), np.sin(arg)]).reshape(2, MEM, LAT, 128).swapaxes(0, 1)
    return (
        wave_x.astype(np.float32),
        wave_z.astype(np.float32),
        phi_high,
        phi_low,
        theta_high,
        theta_low,
    )


def times(a, b):
    return a[0] * b[0] - a[1] * b[1], a[0] * b[1] + a[1] * b[0]


def halves(x):
    high = x.astype(jnp.bfloat16)
    return high, (x - high.astype(jnp.float32)).astype(jnp.bfloat16)


def dot(a, b):
    return jnp.dot(a, b, preferred_element_type=jnp.float32)


def kernel(
    index,
    patterns, operators, wave_x_in, wave_z_in, phi_high_in, phi_low_in, theta_high_in, theta_low_in,
    out,
    own, wide, ops, wave_x, wave_z, phi_high, phi_low, theta_high, theta_low,
    phase, translated, high, low, made, got, thin,
    load_sem, halo_send, halo_recv, send_sem, recv_sem, back_send, back_recv,
):
    group = lax.axis_index("group")
    me = lax.axis_index("member")
    groups = lax.axis_size("group")
    above = lax.rem(group + 1, groups)
    below = lax.rem(group + groups - 1, groups)

    def load(k, src, dst):
        return pltpu.make_async_copy(src, dst, load_sem.at[k])

    loads = [
        load(0, patterns, own),
        load(1, operators, ops),
        load(2, wave_x_in.at[me], wave_x),
        load(3, wave_z_in.at[me], wave_z),
        load(4, patterns, wide.at[pl.ds(BAND, CL)]),
        load(5, phi_high_in, phi_high),
        load(6, phi_low_in, phi_low),
        load(7, theta_high_in, theta_high),
        load(8, theta_low_in, theta_low),
    ]
    for one in loads:
        one.start()

    def other(r):
        y = lax.rem(me // 8 + r // 8, 4)
        x = lax.rem(lax.rem(me // 2, 4) + lax.rem(r // 2, 4), 4)
        c = lax.rem(me + r, 2)
        return y * 8 + x * 2 + c

    barrier = pltpu.get_barrier_semaphore()
    pl.semaphore_signal(barrier, inc=1, device_id=(above, me), device_id_type=MESH)
    pl.semaphore_signal(barrier, inc=1, device_id=(below, me), device_id_type=MESH)

    @pl.loop(1, MEM)
    def _(r):
        pl.semaphore_signal(barrier, inc=1, device_id=(group, other(r)), device_id_type=MESH)

    pl.semaphore_wait(barrier, MEM + 1)

    up = pltpu.make_async_remote_copy(
        src_ref=patterns.at[pl.ds(CL - BAND, BAND)],
        dst_ref=wide.at[pl.ds(0, BAND)],
        send_sem=halo_send.at[0],
        recv_sem=halo_recv.at[0],
        device_id=(above, me),
        device_id_type=MESH,
    )
    down = pltpu.make_async_remote_copy(
        src_ref=patterns.at[pl.ds(0, BAND)],
        dst_ref=wide.at[pl.ds(CL + BAND, BAND)],
        send_sem=halo_send.at[1],
        recv_sem=halo_recv.at[1],
        device_id=(below, me),
        device_id_type=MESH,
    )
    up.start()
    down.start()

    loads[2].wait()
    loads[3].wait()
    x_real, x_imag = wave_x[0], wave_x[1]

    def turned(v):
        return jnp.concatenate([v[:, NP - NP // 4 :], v[:, : NP - NP // 4]], axis=1)

    y_real, y_imag = turned(x_real), turned(x_imag)
    z_real = jnp.concatenate([wave_z[0]] * (NP // 128), axis=1)
    z_imag = jnp.concatenate([wave_z[1]] * (NP // 128), axis=1)
    for octant in range(8):
        sx, sy, sz = 1 - 2 * (octant % 2), 1 - 2 * (octant // 2 % 2), 1 - 2 * (octant // 4)
        xy = times((x_real, sx * x_imag), (y_real, sy * y_imag))
        full = times(xy, (z_real, sz * z_imag))
        phase[octant, 0], phase[octant, 1] = full

    def translate(cluster, cells):
        real = jnp.zeros((LAT, NP), jnp.float32)
        imag = jnp.zeros((LAT, NP), jnp.float32)
        for p in range(NPART):
            cell = cells[index[cluster, p]]
            factor = ops[index[cluster, NPART + p]]
            part = times(factor, cell)
            real, imag = real + part[0], imag + part[1]
        translated[cluster, 0] = real
        translated[cluster, 1] = imag

    loads[0].wait()
    loads[1].wait()

    @pl.loop(BAND, CL - BAND)
    def _(cluster):
        translate(cluster, own)

    for one in loads[4:]:
        one.wait()
    up.wait()
    down.wait()

    @pl.loop(0, 2 * BAND)
    def _(n):
        translate(jnp.where(n < BAND, n, n + CL - 2 * BAND), wide)

    def out_copy(r):
        return pltpu.make_async_remote_copy(
            src_ref=made.at[r],
            dst_ref=got.at[me],
            send_sem=send_sem.at[r],
            recv_sem=recv_sem.at[r],
            device_id=(group, other(r)),
            device_id_type=MESH,
        )

    def shift_and_reduce(first, count):
        @pl.loop(0, count)
        def _(i):
            member = other(lax.rem(first + i, MEM))
            for k in range(PER):
                parent = translated[index[member, 2 * NPART + k]]
                moved = times(parent, phase[index[member, 2 * NPART + PER + k]])
                both = jnp.concatenate(moved, axis=0)
                h, l = halves(both)
                rows = pl.ds(pl.multiple_of((i * PER + k) * 2 * LAT, 2 * LAT), 2 * LAT)
                high[rows, :] = h
                low[rows, :] = l

        total = count * PER * 2 * LAT
        h, l = high[:total, :], low[:total, :]
        result = dot(h, phi_high[...]) + dot(h, phi_low[...]) + dot(l, phi_high[...])
        return result.reshape(count, PER, 2, LAT, NPC)

    part = 8
    for first in range(1, MEM, part):
        block = shift_and_reduce(first, part)
        left = min(part, MEM - first)
        made[first : first + left] = block[:left]
        if left < part:
            got[me] = block[left]

        @pl.loop(first, first + left)
        def _(r):
            out_copy(r).start()

    @pl.loop(1, MEM)
    def _(r):
        out_copy(r).wait()

    for k in range(PER):
        h, l = halves(got[:, k].reshape(MEM * 2 * LAT, NPC))
        result = dot(theta_high[...], h) + dot(theta_low[...], h) + dot(theta_high[...], l)
        thin[:, k] = result.reshape(MEM, 2 * OUT_LAT, NPC)

    def back_copy(r):
        return pltpu.make_async_remote_copy(
            src_ref=thin.at[other(r)],
            dst_ref=out.at[pl.ds(me * PER, PER)],
            send_sem=back_send.at[r],
            recv_sem=back_recv.at[r],
            device_id=(group, other(r)),
            device_id_type=MESH,
        )

    @pl.loop(1, MEM)
    def _(r):
        back_copy(r).start()

    out[pl.ds(me * PER, PER)] = thin[me]

    @pl.loop(1, MEM)
    def _(r):
        back_copy(r).wait()


def on_device(patterns, operators, partners, operator_index, child_parent, child_octant, *, constants):
    f32, bf16 = jnp.float32, jnp.bfloat16
    smem = pl.BlockSpec(memory_space=pltpu.SMEM)
    hbm = pl.BlockSpec(memory_space=pltpu.HBM)
    dma = pltpu.SemaphoreType.DMA
    start = lax.axis_index("group") * CL
    cluster = jnp.arange(CL)[:, None]
    inner = (cluster >= BAND) & (cluster < CL - BAND)
    index = jnp.concatenate(
        [
            partners - start + jnp.where(inner, 0, BAND),
            operator_index,
            child_parent.reshape(MEM, PER) - start,
            child_octant.reshape(MEM, PER),
        ],
        axis=1,
    )
    result = pl.pallas_call(
        kernel,
        out_shape=jax.ShapeDtypeStruct((CH, 2 * OUT_LAT, NPC), f32),
        in_specs=[smem] + [hbm] * (2 + len(constants)),
        out_specs=pl.BlockSpec(memory_space=pltpu.VMEM),
        scratch_shapes=[
            pltpu.VMEM((CL, 2, LAT, NP), f32),
            pltpu.VMEM((CL + 2 * BAND, 2, LAT, NP), f32),
            pltpu.VMEM(operators.shape, f32),
            pltpu.VMEM((2, LAT, NP), f32),
            pltpu.VMEM((2, LAT, 128), f32),
            pltpu.VMEM((NP, NPC), bf16),
            pltpu.VMEM((NP, NPC), bf16),
            pltpu.VMEM((2 * NTC, 2 * NT), bf16),
            pltpu.VMEM((2 * NTC, 2 * NT), bf16),
            pltpu.VMEM((8, 2, LAT, NP), f32),
            pltpu.VMEM((CL, 2, LAT, NP), f32),
            pltpu.VMEM((256, NP), bf16),
            pltpu.VMEM((256, NP), bf16),
            pltpu.VMEM((MEM, PER, 2, LAT, NPC), f32),
            pltpu.VMEM((MEM, PER, 2, LAT, NPC), f32),
            pltpu.VMEM((MEM, PER, 2 * OUT_LAT, NPC), f32),
            dma((9,)),
            dma((2,)),
            dma((2,)),
            dma((MEM,)),
            dma((MEM,)),
            dma((MEM,)),
            dma((MEM,)),
        ],
        compiler_params=pltpu.CompilerParams(
            collective_id=0, has_side_effects=True, vmem_limit_bytes=40 * 2**20
        ),
        cost_estimate=pl.CostEstimate(flops=10**9, bytes_accessed=6 * 2**20, transcendentals=0),
    )(index, patterns, operators, *constants)
    return result.reshape(CH, 2, OUT_LAT, NPC)


def solution(mesh):
    constants = tables()
    whole = P("group", None, "member", None)
    return jax.shard_map(
        functools.partial(on_device, constants=constants),
        mesh=mesh,
        in_specs=(whole, P(None, None, "member", None), P("group", None), P("group", None), P("group"), P("group")),
        out_specs=whole,
        check_vma=False,
    )
```

```python
import functools

import jax
import jax.numpy as jnp
import ml_dtypes
import numpy as np
from jax import lax
from jax.experimental import pallas as pl
from jax.experimental.pallas import tpu as pltpu
from jax.sharding import PartitionSpec as P

MESH = pl.DeviceIdType.MESH

NT, NP, NTC, NPC = 256, 512, 128, 256
NPART = 8
CL = 32
CH = 64
BAND = 8
MEM = 32
LAT = NT // MEM
OUT_LAT = NTC // MEM
PER = CH // MEM
REACH = 6.0


def split(values):
    high = values.astype(ml_dtypes.bfloat16)
    low = (values - high.astype(np.float64)).astype(ml_dtypes.bfloat16)
    return high, low


def tables():
    theta_fine = np.pi * (np.arange(NT) + 0.5) / NT
    theta_coarse = np.pi * (np.arange(NTC) + 0.5) / NTC
    orders = np.arange(NTC)
    weights = np.where(orders > 0, 2.0, 1.0)
    theta = (np.cos(np.outer(theta_coarse, orders)) * weights) @ np.cos(np.outer(theta_fine, orders)).T / NT
    phi_fine = 2.0 * np.pi * np.arange(NP) / NP
    phi_coarse = 2.0 * np.pi * np.arange(NPC) / NPC
    modes = np.arange(NPC // 2 + 1)
    mode_weights = np.where((modes > 0) & (modes < NPC // 2), 2.0, 1.0)
    phi = (
        (np.cos(np.outer(phi_coarse, modes)) * mode_weights) @ np.cos(np.outer(phi_fine, modes)).T
        + (np.sin(np.outer(phi_coarse, modes)) * mode_weights) @ np.sin(np.outer(phi_fine, modes)).T
    ) / NP
    big = np.zeros((MEM, 2, OUT_LAT, MEM, 2, LAT))
    blocks = theta.reshape(MEM, OUT_LAT, MEM, LAT)
    for part in range(2):
        big[:, part, :, :, part, :] = blocks
    theta_high, theta_low = split(big.reshape(MEM * 2 * OUT_LAT, MEM * 2 * LAT))
    phi_high, phi_low = split(phi.T)
    arg = REACH * np.sin(theta_fine)[:, None] * np.cos(phi_fine)[None, :]
    wave_x = np.stack([np.cos(arg), np.sin(arg)]).reshape(2, MEM, LAT, NP).swapaxes(0, 1)
    arg = np.broadcast_to(REACH * np.cos(theta_fine)[:, None], (NT, 128))
    wave_z = np.stack([np.cos(arg), np.sin(arg)]).reshape(2, MEM, LAT, 128).swapaxes(0, 1)
    return (
        wave_x.astype(np.float32),
        wave_z.astype(np.float32),
        phi_high,
        phi_low,
        theta_high,
        theta_low,
    )


def times(a, b):
    return a[0] * b[0] - a[1] * b[1], a[0] * b[1] + a[1] * b[0]


def halves(x):
    high = x.astype(jnp.bfloat16)
    return high, (x - high.astype(jnp.float32)).astype(jnp.bfloat16)


def dot(a, b):
    return jnp.dot(a, b, preferred_element_type=jnp.float32)


def kernel(
    partners_in, factors_in, parents_in, octants_in, patterns, operators, wave_x_in, wave_z_in, phi_high_in, phi_low_in, theta_high_in, theta_low_in,
    out,
    partners, factors, parents, octants,
    own, wide, ops, wave_x, wave_z, phi_high, phi_low, theta_high, theta_low,
    phase, translated, high, low, made, got, thin,
    load_sem, halo_send, halo_recv, send_sem, recv_sem, back_send, back_recv,
):
    group = lax.axis_index("group")
    me = lax.axis_index("member")
    groups = lax.axis_size("group")
    above = lax.rem(group + 1, groups)
    below = lax.rem(group + groups - 1, groups)

    def load(k, src, dst):
        return pltpu.make_async_copy(src, dst, load_sem.at[k])

    loads = [
        load(0, wave_x_in.at[me], wave_x),
        load(1, wave_z_in.at[me], wave_z),
        load(2, partners_in, partners),
        load(3, factors_in, factors),
        load(4, patterns, own),
        load(5, operators, ops),
        load(6, patterns, wide.at[pl.ds(BAND, CL)]),
        load(7, parents_in, parents),
        load(8, octants_in, octants),
        load(9, phi_high_in, phi_high),
        load(10, phi_low_in, phi_low),
        load(11, theta_high_in, theta_high),
        load(12, theta_low_in, theta_low),
    ]
    for one in loads:
        one.start()

    def other(r):
        y = lax.rem(me // 8 + r // 8, 4)
        x = lax.rem(lax.rem(me // 2, 4) + lax.rem(r // 2, 4), 4)
        c = lax.rem(me + r, 2)
        return y * 8 + x * 2 + c

    barrier = pltpu.get_barrier_semaphore()
    pl.semaphore_signal(barrier, inc=1, device_id=(above, me), device_id_type=MESH)
    pl.semaphore_signal(barrier, inc=1, device_id=(below, me), device_id_type=MESH)

    @pl.loop(1, MEM)
    def _(r):
        pl.semaphore_signal(barrier, inc=1, device_id=(group, other(r)), device_id_type=MESH)

    pl.semaphore_wait(barrier, MEM + 1)

    up = pltpu.make_async_remote_copy(
        src_ref=patterns.at[pl.ds(CL - BAND, BAND)],
        dst_ref=wide.at[pl.ds(0, BAND)],
        send_sem=halo_send.at[0],
        recv_sem=halo_recv.at[0],
        device_id=(above, me),
        device_id_type=MESH,
    )
    down = pltpu.make_async_remote_copy(
        src_ref=patterns.at[pl.ds(0, BAND)],
        dst_ref=wide.at[pl.ds(CL + BAND, BAND)],
        send_sem=halo_send.at[1],
        recv_sem=halo_recv.at[1],
        device_id=(below, me),
        device_id_type=MESH,
    )
    up.start()
    down.start()

    for one in loads[:2]:
        one.wait()
    x_real, x_imag = wave_x[0], wave_x[1]

    def turned(v):
        return jnp.concatenate([v[:, NP - NP // 4 :], v[:, : NP - NP // 4]], axis=1)

    y_real, y_imag = turned(x_real), turned(x_imag)
    z_real = jnp.concatenate([wave_z[0]] * (NP // 128), axis=1)
    z_imag = jnp.concatenate([wave_z[1]] * (NP // 128), axis=1)
    for octant in range(8):
        sx, sy, sz = 1 - 2 * (octant % 2), 1 - 2 * (octant // 2 % 2), 1 - 2 * (octant // 4)
        xy = times((x_real, sx * x_imag), (y_real, sy * y_imag))
        full = times(xy, (z_real, sz * z_imag))
        phase[octant, 0], phase[octant, 1] = full

    def translate(cluster, cells, first):
        real = jnp.zeros((LAT, NP), jnp.float32)
        imag = jnp.zeros((LAT, NP), jnp.float32)
        for p in range(NPART):
            cell = cells[jnp.clip(partners[p, cluster] - first, 0, cells.shape[0] - 1)]
            factor = ops[factors[p, cluster]]
            part = times(factor, cell)
            real, imag = real + part[0], imag + part[1]
        translated[cluster, 0] = real
        translated[cluster, 1] = imag

    for one in loads[2:6]:
        one.wait()

    @pl.loop(BAND, CL - BAND)
    def _(cluster):
        translate(cluster, own, group * CL)

    for one in loads[6:]:
        one.wait()
    up.wait()
    down.wait()

    @pl.loop(0, 2 * BAND)
    def _(n):
        translate(jnp.where(n < BAND, n, n + CL - 2 * BAND), wide, group * CL - BAND)

    def out_copy(r):
        return pltpu.make_async_remote_copy(
            src_ref=made.at[r],
            dst_ref=got.at[me],
            send_sem=send_sem.at[r],
            recv_sem=recv_sem.at[r],
            device_id=(group, other(r)),
            device_id_type=MESH,
        )

    def shift_and_reduce(first, count):
        @pl.loop(0, count)
        def _(i):
            member = other(lax.rem(first + i, MEM))
            for k in range(PER):
                child = member * PER + k
                parent = translated[lax.rem(parents[child], CL)]
                moved = times(parent, phase[octants[child]])
                both = jnp.concatenate(moved, axis=0)
                h, l = halves(both)
                rows = pl.ds(pl.multiple_of((i * PER + k) * 2 * LAT, 2 * LAT), 2 * LAT)
                high[rows, :] = h
                low[rows, :] = l

        total = count * PER * 2 * LAT
        h, l = high[:total, :], low[:total, :]
        result = dot(h, phi_high[...]) + dot(h, phi_low[...]) + dot(l, phi_high[...])
        return result.reshape(count, PER, 2, LAT, NPC)

    part = 8
    for first in range(1, MEM, part):
        block = shift_and_reduce(first, part)
        left = min(part, MEM - first)
        made[first : first + left] = block[:left]
        if left < part:
            got[me] = block[left]

        @pl.loop(first, first + left)
        def _(r):
            out_copy(r).start()

    @pl.loop(1, MEM)
    def _(r):
        out_copy(r).wait()

    for k in range(PER):
        h, l = halves(got[:, k].reshape(MEM * 2 * LAT, NPC))
        result = dot(theta_high[...], h) + dot(theta_low[...], h) + dot(theta_high[...], l)
        thin[:, k] = result.reshape(MEM, 2 * OUT_LAT, NPC)

    def back_copy(r):
        return pltpu.make_async_remote_copy(
            src_ref=thin.at[other(r)],
            dst_ref=out.at[pl.ds(me * PER, PER)],
            send_sem=back_send.at[r],
            recv_sem=back_recv.at[r],
            device_id=(group, other(r)),
            device_id_type=MESH,
        )

    @pl.loop(1, MEM)
    def _(r):
        back_copy(r).start()

    out[pl.ds(me * PER, PER)] = thin[me]

    @pl.loop(1, MEM)
    def _(r):
        back_copy(r).wait()


def on_device(patterns, operators, partners, operator_index, child_parent, child_octant, *, constants):
    f32, bf16 = jnp.float32, jnp.bfloat16
    hbm = pl.BlockSpec(memory_space=pltpu.HBM)
    dma = pltpu.SemaphoreType.DMA
    result = pl.pallas_call(
        kernel,
        out_shape=jax.ShapeDtypeStruct((CH, 2 * OUT_LAT, NPC), f32),
        in_specs=[hbm] * (6 + len(constants)),
        out_specs=pl.BlockSpec(memory_space=pltpu.VMEM),
        scratch_shapes=[
            pltpu.SMEM((NPART, CL), jnp.int32),
            pltpu.SMEM((NPART, CL), jnp.int32),
            pltpu.SMEM((CH,), jnp.int32),
            pltpu.SMEM((CH,), jnp.int32),
            pltpu.VMEM((CL, 2, LAT, NP), f32),
            pltpu.VMEM((CL + 2 * BAND, 2, LAT, NP), f32),
            pltpu.VMEM(operators.shape, f32),
            pltpu.VMEM((2, LAT, NP), f32),
            pltpu.VMEM((2, LAT, 128), f32),
            pltpu.VMEM((NP, NPC), bf16),
            pltpu.VMEM((NP, NPC), bf16),
            pltpu.VMEM((2 * NTC, 2 * NT), bf16),
            pltpu.VMEM((2 * NTC, 2 * NT), bf16),
            pltpu.VMEM((8, 2, LAT, NP), f32),
            pltpu.VMEM((CL, 2, LAT, NP), f32),
            pltpu.VMEM((256, NP), bf16),
            pltpu.VMEM((256, NP), bf16),
            pltpu.VMEM((MEM, PER, 2, LAT, NPC), f32),
            pltpu.VMEM((MEM, PER, 2, LAT, NPC), f32),
            pltpu.VMEM((MEM, PER, 2 * OUT_LAT, NPC), f32),
            dma((13,)),
            dma((2,)),
            dma((2,)),
            dma((MEM,)),
            dma((MEM,)),
            dma((MEM,)),
            dma((MEM,)),
        ],
        compiler_params=pltpu.CompilerParams(
            collective_id=0, has_side_effects=True, vmem_limit_bytes=60 * 2**20
        ),
        cost_estimate=pl.CostEstimate(flops=10**9, bytes_accessed=6 * 2**20, transcendentals=0),
    )(partners.T, operator_index.T, child_parent, child_octant, patterns, operators, *constants)
    return result.reshape(CH, 2, OUT_LAT, NPC)


def solution(mesh):
    constants = tables()
    whole = P("group", None, "member", None)
    return jax.shard_map(
        functools.partial(on_device, constants=constants),
        mesh=mesh,
        in_specs=(whole, P(None, None, "member", None), P("group", None), P("group", None), P("group"), P("group")),
        out_specs=whole,
        check_vma=False,
    )
```

```python
import functools

import jax
import jax.numpy as jnp
import ml_dtypes
import numpy as np
from jax import lax
from jax.experimental import pallas as pl
from jax.experimental.pallas import tpu as pltpu
from jax.sharding import PartitionSpec as P

MESH = pl.DeviceIdType.MESH

NT, NP, NTC, NPC = 256, 512, 128, 256
NPART = 8
CL = 32
CH = 64
BAND = 8
MEM = 32
LAT = NT // MEM
OUT_LAT = NTC // MEM
PER = CH // MEM
REACH = 6.0
HALO_PARTS = 1


def split(values):
    high = values.astype(ml_dtypes.bfloat16)
    low = (values - high.astype(np.float64)).astype(ml_dtypes.bfloat16)
    return high, low


def tables():
    theta_fine = np.pi * (np.arange(NT) + 0.5) / NT
    theta_coarse = np.pi * (np.arange(NTC) + 0.5) / NTC
    orders = np.arange(NTC)
    weights = np.where(orders > 0, 2.0, 1.0)
    theta = (np.cos(np.outer(theta_coarse, orders)) * weights) @ np.cos(np.outer(theta_fine, orders)).T / NT
    phi_fine = 2.0 * np.pi * np.arange(NP) / NP
    phi_coarse = 2.0 * np.pi * np.arange(NPC) / NPC
    modes = np.arange(NPC // 2 + 1)
    mode_weights = np.where((modes > 0) & (modes < NPC // 2), 2.0, 1.0)
    phi = (
        (np.cos(np.outer(phi_coarse, modes)) * mode_weights) @ np.cos(np.outer(phi_fine, modes)).T
        + (np.sin(np.outer(phi_coarse, modes)) * mode_weights) @ np.sin(np.outer(phi_fine, modes)).T
    ) / NP
    big = np.zeros((MEM, 2, OUT_LAT, MEM, 2, LAT))
    blocks = theta.reshape(MEM, OUT_LAT, MEM, LAT)
    for part in range(2):
        big[:, part, :, :, part, :] = blocks
    theta_high, theta_low = split(big.reshape(MEM * 2 * OUT_LAT, MEM * 2 * LAT))
    phi_high, phi_low = split(phi.T)
    arg = REACH * np.sin(theta_fine)[:, None] * np.cos(phi_fine)[None, :]
    wave_x = np.stack([np.cos(arg), np.sin(arg)]).reshape(2, MEM, LAT, NP).swapaxes(0, 1)
    arg = np.broadcast_to(REACH * np.cos(theta_fine)[:, None], (NT, 128))
    wave_z = np.stack([np.cos(arg), np.sin(arg)]).reshape(2, MEM, LAT, 128).swapaxes(0, 1)
    return (
        wave_x.astype(np.float32),
        wave_z.astype(np.float32),
        phi_high,
        phi_low,
        theta_high,
        theta_low,
    )


def times(a, b):
    return a[0] * b[0] - a[1] * b[1], a[0] * b[1] + a[1] * b[0]


def halves(x):
    high = x.astype(jnp.bfloat16)
    return high, (x - high.astype(jnp.float32)).astype(jnp.bfloat16)


def dot(a, b):
    return jnp.dot(a, b, preferred_element_type=jnp.float32)


def kernel(
    partners_in, factors_in, parents_in, octants_in, patterns, operators, wave_x_in, wave_z_in, phi_high_in, phi_low_in, theta_high_in, theta_low_in,
    out,
    partners, factors, parents, octants,
    own, wide, ops, wave_x, wave_z, phi_high, phi_low, theta_high, theta_low,
    phase, translated, high, low, made, got, thin,
    load_sem, halo_send, halo_recv, send_sem, recv_sem, back_send, back_recv,
):
    group = lax.axis_index("group")
    me = lax.axis_index("member")
    groups = lax.axis_size("group")
    below, above = group - 1, group + 1
    has_below, has_above = group > 0, group < groups - 1

    def load(k, src, dst):
        return pltpu.make_async_copy(src, dst, load_sem.at[k])

    loads = [
        load(0, wave_x_in.at[me], wave_x),
        load(1, wave_z_in.at[me], wave_z),
        load(2, partners_in, partners),
        load(3, factors_in, factors),
        load(4, patterns, own),
        load(5, operators, ops),
        load(6, patterns, wide.at[pl.ds(BAND, CL)]),
        load(7, parents_in, parents),
        load(8, octants_in, octants),
        load(9, phi_high_in, phi_high),
        load(10, phi_low_in, phi_low),
        load(11, theta_high_in, theta_high),
        load(12, theta_low_in, theta_low),
    ]
    for one in loads:
        one.start()

    def other(r):
        y = lax.rem(me // 8 + r // 8, 4)
        x = lax.rem(lax.rem(me // 2, 4) + lax.rem(r // 2, 4), 4)
        c = lax.rem(me + r, 2)
        return y * 8 + x * 2 + c

    barrier = pltpu.get_barrier_semaphore()

    @pl.when(has_above)
    def _():
        pl.semaphore_signal(barrier, inc=1, device_id=(above, me), device_id_type=MESH)

    @pl.when(has_below)
    def _():
        pl.semaphore_signal(barrier, inc=1, device_id=(below, me), device_id_type=MESH)

    @pl.loop(1, MEM)
    def _(r):
        pl.semaphore_signal(barrier, inc=1, device_id=(group, other(r)), device_id_type=MESH)

    for one in loads[:2]:
        one.wait()
    x_real, x_imag = wave_x[0], wave_x[1]

    def turned(v):
        return jnp.concatenate([v[:, NP - NP // 4 :], v[:, : NP - NP // 4]], axis=1)

    y_real, y_imag = turned(x_real), turned(x_imag)
    z_real = jnp.concatenate([wave_z[0]] * (NP // 128), axis=1)
    z_imag = jnp.concatenate([wave_z[1]] * (NP // 128), axis=1)
    for octant in range(8):
        sx, sy, sz = 1 - 2 * (octant % 2), 1 - 2 * (octant // 2 % 2), 1 - 2 * (octant // 4)
        xy = times((x_real, sx * x_imag), (y_real, sy * y_imag))
        full = times(xy, (z_real, sz * z_imag))
        phase[octant, 0], phase[octant, 1] = full

    def translate(cluster, cells, first):
        real = jnp.zeros((LAT, NP), jnp.float32)
        imag = jnp.zeros((LAT, NP), jnp.float32)
        for p in range(NPART):
            cell = cells[jnp.clip(partners[p, cluster] - first, 0, cells.shape[0] - 1)]
            factor = ops[factors[p, cluster]]
            part = times(factor, cell)
            real, imag = real + part[0], imag + part[1]
        translated[cluster, 0] = real
        translated[cluster, 1] = imag

    for one in loads[2:6]:
        one.wait()

    @pl.loop(BAND, CL - BAND)
    def _(cluster):
        translate(cluster, own, group * CL)

    pl.semaphore_wait(barrier, MEM - 1 + jnp.minimum(group, 1) + jnp.minimum(groups - 1 - group, 1))

    width = BAND // HALO_PARTS

    def up(n, to):
        return pltpu.make_async_remote_copy(
            src_ref=patterns.at[pl.ds(CL - BAND + n * width, width)],
            dst_ref=wide.at[pl.ds(n * width, width)],
            send_sem=halo_send.at[0, n],
            recv_sem=halo_recv.at[0, n],
            device_id=(to, me),
            device_id_type=MESH,
        )

    def down(n, to):
        return pltpu.make_async_remote_copy(
            src_ref=patterns.at[pl.ds(n * width, width)],
            dst_ref=wide.at[pl.ds(CL + BAND + n * width, width)],
            send_sem=halo_send.at[1, n],
            recv_sem=halo_recv.at[1, n],
            device_id=(to, me),
            device_id_type=MESH,
        )

    for n in range(HALO_PARTS):

        @pl.when(has_above)
        def _():
            up(n, above).start()

        @pl.when(has_below)
        def _():
            down(n, below).start()

    for one in loads[6:]:
        one.wait()
    for n in range(HALO_PARTS):

        @pl.when(has_above)
        def _():
            up(n, above).wait_send()
            down(n, above).wait_recv()

        @pl.when(has_below)
        def _():
            down(n, below).wait_send()
            up(n, below).wait_recv()

    @pl.loop(0, 2 * BAND)
    def _(n):
        translate(jnp.where(n < BAND, n, n + CL - 2 * BAND), wide, group * CL - BAND)

    def out_copy(r):
        return pltpu.make_async_remote_copy(
            src_ref=made.at[r],
            dst_ref=got.at[me],
            send_sem=send_sem.at[r],
            recv_sem=recv_sem.at[r],
            device_id=(group, other(r)),
            device_id_type=MESH,
        )

    def shift_and_reduce(first, count):
        @pl.loop(0, count)
        def _(i):
            member = other(lax.rem(first + i, MEM))
            for k in range(PER):
                child = member * PER + k
                parent = translated[lax.rem(parents[child], CL)]
                moved = times(parent, phase[octants[child]])
                both = jnp.concatenate(moved, axis=0)
                h, l = halves(both)
                rows = pl.ds(pl.multiple_of((i * PER + k) * 2 * LAT, 2 * LAT), 2 * LAT)
                high[rows, :] = h
                low[rows, :] = l

        total = count * PER * 2 * LAT
        h, l = high[:total, :], low[:total, :]
        result = dot(h, phi_high[...]) + dot(h, phi_low[...]) + dot(l, phi_high[...])
        return result.reshape(count, PER, 2, LAT, NPC)

    part = 8
    for first in range(1, MEM, part):
        block = shift_and_reduce(first, part)
        left = min(part, MEM - first)
        made[first : first + left] = block[:left]
        if left < part:
            got[me] = block[left]

        @pl.loop(first, first + left)
        def _(r):
            out_copy(r).start()

    @pl.loop(1, MEM)
    def _(r):
        out_copy(r).wait()

    for k in range(PER):
        h, l = halves(got[:, k].reshape(MEM * 2 * LAT, NPC))
        result = dot(theta_high[...], h) + dot(theta_low[...], h) + dot(theta_high[...], l)
        thin[:, k] = result.reshape(MEM, 2 * OUT_LAT, NPC)

    def back_copy(r):
        return pltpu.make_async_remote_copy(
            src_ref=thin.at[other(r)],
            dst_ref=out.at[pl.ds(me * PER, PER)],
            send_sem=back_send.at[r],
            recv_sem=back_recv.at[r],
            device_id=(group, other(r)),
            device_id_type=MESH,
        )

    @pl.loop(1, MEM)
    def _(r):
        back_copy(r).start()

    out[pl.ds(me * PER, PER)] = thin[me]

    @pl.loop(1, MEM)
    def _(r):
        back_copy(r).wait()


def on_device(patterns, operators, partners, operator_index, child_parent, child_octant, *, constants):
    f32, bf16 = jnp.float32, jnp.bfloat16
    hbm = pl.BlockSpec(memory_space=pltpu.HBM)
    dma = pltpu.SemaphoreType.DMA
    result = pl.pallas_call(
        kernel,
        out_shape=jax.ShapeDtypeStruct((CH, 2 * OUT_LAT, NPC), f32),
        in_specs=[hbm] * (6 + len(constants)),
        out_specs=pl.BlockSpec(memory_space=pltpu.VMEM),
        scratch_shapes=[
            pltpu.SMEM((NPART, CL), jnp.int32),
            pltpu.SMEM((NPART, CL), jnp.int32),
            pltpu.SMEM((CH,), jnp.int32),
            pltpu.SMEM((CH,), jnp.int32),
            pltpu.VMEM((CL, 2, LAT, NP), f32),
            pltpu.VMEM((CL + 2 * BAND, 2, LAT, NP), f32),
            pltpu.VMEM(operators.shape, f32),
            pltpu.VMEM((2, LAT, NP), f32),
            pltpu.VMEM((2, LAT, 128), f32),
            pltpu.VMEM((NP, NPC), bf16),
            pltpu.VMEM((NP, NPC), bf16),
            pltpu.VMEM((2 * NTC, 2 * NT), bf16),
            pltpu.VMEM((2 * NTC, 2 * NT), bf16),
            pltpu.VMEM((8, 2, LAT, NP), f32),
            pltpu.VMEM((CL, 2, LAT, NP), f32),
            pltpu.VMEM((256, NP), bf16),
            pltpu.VMEM((256, NP), bf16),
            pltpu.VMEM((MEM, PER, 2, LAT, NPC), f32),
            pltpu.VMEM((MEM, PER, 2, LAT, NPC), f32),
            pltpu.VMEM((MEM, PER, 2 * OUT_LAT, NPC), f32),
            dma((13,)),
            dma((2, HALO_PARTS)),
            dma((2, HALO_PARTS)),
            dma((MEM,)),
            dma((MEM,)),
            dma((MEM,)),
            dma((MEM,)),
        ],
        compiler_params=pltpu.CompilerParams(
            collective_id=0, has_side_effects=True, vmem_limit_bytes=60 * 2**20
        ),
        cost_estimate=pl.CostEstimate(flops=10**9, bytes_accessed=6 * 2**20, transcendentals=0),
    )(partners.T, operator_index.T, child_parent, child_octant, patterns, operators, *constants)
    return result.reshape(CH, 2, OUT_LAT, NPC)


def solution(mesh):
    constants = tables()
    whole = P("group", None, "member", None)
    return jax.shard_map(
        functools.partial(on_device, constants=constants),
        mesh=mesh,
        in_specs=(whole, P(None, None, "member", None), P("group", None), P("group", None), P("group"), P("group")),
        out_specs=whole,
        check_vma=False,
    )
```

```python
import functools

import jax
import jax.numpy as jnp
import ml_dtypes
import numpy as np
from jax import lax
from jax.experimental import pallas as pl
from jax.experimental.pallas import tpu as pltpu
from jax.sharding import PartitionSpec as P

MESH = pl.DeviceIdType.MESH

NT, NP, NTC, NPC = 256, 512, 128, 256
NPART = 8
CL = 32
CH = 64
BAND = 8
MEM = 32
LAT = NT // MEM
OUT_LAT = NTC // MEM
PER = CH // MEM
REACH = 6.0
HALO_PARTS = 1
PART = 8
STEPS = sorted(
    ((y, x, core) for y in range(4) for x in range(4) for core in range(2)),
    key=lambda step: (step == (0, 0, 0), -min(step[0], 4 - step[0]) - min(step[1], 4 - step[1])),
)


def split(values):
    high = values.astype(ml_dtypes.bfloat16)
    low = (values - high.astype(np.float64)).astype(ml_dtypes.bfloat16)
    return high, low


def tables():
    theta_fine = np.pi * (np.arange(NT) + 0.5) / NT
    theta_coarse = np.pi * (np.arange(NTC) + 0.5) / NTC
    orders = np.arange(NTC)
    weights = np.where(orders > 0, 2.0, 1.0)
    theta = (np.cos(np.outer(theta_coarse, orders)) * weights) @ np.cos(np.outer(theta_fine, orders)).T / NT
    phi_fine = 2.0 * np.pi * np.arange(NP) / NP
    phi_coarse = 2.0 * np.pi * np.arange(NPC) / NPC
    modes = np.arange(NPC // 2 + 1)
    mode_weights = np.where((modes > 0) & (modes < NPC // 2), 2.0, 1.0)
    phi = (
        (np.cos(np.outer(phi_coarse, modes)) * mode_weights) @ np.cos(np.outer(phi_fine, modes)).T
        + (np.sin(np.outer(phi_coarse, modes)) * mode_weights) @ np.sin(np.outer(phi_fine, modes)).T
    ) / NP
    big = np.zeros((MEM, 2, OUT_LAT, MEM, 2, LAT))
    blocks = theta.reshape(MEM, OUT_LAT, MEM, LAT)
    for part in range(2):
        big[:, part, :, :, part, :] = blocks
    theta_high, theta_low = split(big.reshape(MEM * 2 * OUT_LAT, MEM * 2 * LAT))
    phi_high, phi_low = split(phi.T)
    arg = REACH * np.sin(theta_fine)[:, None] * np.cos(phi_fine)[None, :]
    wave_x = np.stack([np.cos(arg), np.sin(arg)]).reshape(2, MEM, LAT, NP).swapaxes(0, 1)
    arg = np.broadcast_to(REACH * np.cos(theta_fine)[:, None], (NT, 128))
    wave_z = np.stack([np.cos(arg), np.sin(arg)]).reshape(2, MEM, LAT, 128).swapaxes(0, 1)
    return (
        wave_x.astype(np.float32),
        wave_z.astype(np.float32),
        phi_high,
        phi_low,
        theta_high,
        theta_low,
    )


def times(a, b):
    return a[0] * b[0] - a[1] * b[1], a[0] * b[1] + a[1] * b[0]


def halves(x):
    high = x.astype(jnp.bfloat16)
    return high, (x - high.astype(jnp.float32)).astype(jnp.bfloat16)


def dot(a, b):
    return jnp.dot(a, b, preferred_element_type=jnp.float32)


def kernel(
    partners_in, factors_in, parents_in, octants_in, patterns, operators, wave_x_in, wave_z_in, phi_high_in, phi_low_in, theta_high_in, theta_low_in,
    out,
    partners, factors, parents, octants,
    own, wide, ops, wave_x, wave_z, phi_high, phi_low, theta_high, theta_low,
    phase, translated, high, low, made, got, thin,
    load_sem, halo_send, halo_recv, send_sem, recv_sem, back_send, back_recv, turn,
):
    group = lax.axis_index("group")
    me = lax.axis_index("member")
    groups = lax.axis_size("group")
    below, above = group - 1, group + 1
    has_below, has_above = group > 0, group < groups - 1

    def load(k, src, dst):
        return pltpu.make_async_copy(src, dst, load_sem.at[k])

    loads = [
        load(0, wave_x_in.at[me], wave_x),
        load(1, wave_z_in.at[me], wave_z),
        load(2, partners_in, partners),
        load(3, factors_in, factors),
        load(4, patterns, own),
        load(5, operators, ops),
        load(6, patterns, wide.at[pl.ds(BAND, CL)]),
        load(7, parents_in, parents),
        load(8, octants_in, octants),
        load(9, phi_high_in, phi_high),
        load(10, phi_low_in, phi_low),
        load(11, theta_high_in, theta_high),
        load(12, theta_low_in, theta_low),
    ]
    for one in loads:
        one.start()

    ys = [lax.rem(me // 8 + step, 4) * 8 for step in range(4)]
    xs = [lax.rem(me // 2 + step, 4) * 2 for step in range(4)]
    cores = [lax.rem(me + step, 2) for step in range(2)]
    others = [ys[y] + xs[x] + cores[core] for y, x, core in STEPS]

    barrier = pltpu.get_barrier_semaphore()

    @pl.when(has_above)
    def _():
        pl.semaphore_signal(barrier, inc=1, device_id=(above, me), device_id_type=MESH)

    @pl.when(has_below)
    def _():
        pl.semaphore_signal(barrier, inc=1, device_id=(below, me), device_id_type=MESH)

    for member in others[: MEM - 1]:
        pl.semaphore_signal(barrier, inc=1, device_id=(group, member), device_id_type=MESH)

    for one in loads[:2]:
        one.wait()
    x_real, x_imag = wave_x[0], wave_x[1]

    def turned(v):
        return jnp.concatenate([v[:, NP - NP // 4 :], v[:, : NP - NP // 4]], axis=1)

    y_real, y_imag = turned(x_real), turned(x_imag)
    z_real = jnp.concatenate([wave_z[0]] * (NP // 128), axis=1)
    z_imag = jnp.concatenate([wave_z[1]] * (NP // 128), axis=1)
    for octant in range(8):
        sx, sy, sz = 1 - 2 * (octant % 2), 1 - 2 * (octant // 2 % 2), 1 - 2 * (octant // 4)
        xy = times((x_real, sx * x_imag), (y_real, sy * y_imag))
        full = times(xy, (z_real, sz * z_imag))
        phase[octant, 0], phase[octant, 1] = full

    def translate(cluster, cells, first):
        real = jnp.zeros((LAT, NP), jnp.float32)
        imag = jnp.zeros((LAT, NP), jnp.float32)
        for p in range(NPART):
            cell = cells[jnp.clip(partners[p, cluster] - first, 0, cells.shape[0] - 1)]
            factor = ops[factors[p, cluster]]
            part = times(factor, cell)
            real, imag = real + part[0], imag + part[1]
        translated[cluster, 0] = real
        translated[cluster, 1] = imag

    for one in loads[2:6]:
        one.wait()

    @pl.loop(BAND, CL - BAND)
    def _(cluster):
        translate(cluster, own, group * CL)

    pl.semaphore_wait(barrier, MEM - 1 + jnp.minimum(group, 1) + jnp.minimum(groups - 1 - group, 1))

    @pl.when(lax.rem(me, 2) == 1)
    def _():
        pl.semaphore_wait(turn, 1)

    width = BAND // HALO_PARTS

    def up(n, to):
        return pltpu.make_async_remote_copy(
            src_ref=patterns.at[pl.ds(CL - BAND + n * width, width)],
            dst_ref=wide.at[pl.ds(n * width, width)],
            send_sem=halo_send.at[0, n],
            recv_sem=halo_recv.at[0, n],
            device_id=(to, me),
            device_id_type=MESH,
        )

    def down(n, to):
        return pltpu.make_async_remote_copy(
            src_ref=patterns.at[pl.ds(n * width, width)],
            dst_ref=wide.at[pl.ds(CL + BAND + n * width, width)],
            send_sem=halo_send.at[1, n],
            recv_sem=halo_recv.at[1, n],
            device_id=(to, me),
            device_id_type=MESH,
        )

    for n in range(HALO_PARTS):

        @pl.when(has_above)
        def _():
            up(n, above).start()

        @pl.when(has_below)
        def _():
            down(n, below).start()

    for one in loads[6:]:
        one.wait()
    for n in range(HALO_PARTS):

        @pl.when(has_above)
        def _():
            up(n, above).wait_send()

        @pl.when(has_below)
        def _():
            down(n, below).wait_send()

    @pl.when(lax.rem(me, 2) == 0)
    def _():
        pl.semaphore_signal(turn, inc=1, device_id=(group, ys[0] + xs[0] + cores[1]), device_id_type=MESH)

    for n in range(HALO_PARTS):

        @pl.when(has_above)
        def _():
            down(n, above).wait_recv()

        @pl.when(has_below)
        def _():
            up(n, below).wait_recv()

    @pl.loop(0, 2 * BAND)
    def _(n):
        translate(jnp.where(n < BAND, n, n + CL - 2 * BAND), wide, group * CL - BAND)

    def shift_and_reduce(k, members):
        for i, member in enumerate(members):
            child = member * PER + k
            parent = translated[lax.rem(parents[child], CL)]
            moved = times(parent, phase[octants[child]])
            both = jnp.concatenate(moved, axis=0)
            h, l = halves(both)
            rows = slice(i * 2 * LAT, (i + 1) * 2 * LAT)
            high[rows, :] = h
            low[rows, :] = l
        total = len(members) * 2 * LAT
        h, l = high[:total, :], low[:total, :]
        result = dot(h, phi_high[...]) + dot(h, phi_low[...]) + dot(l, phi_high[...])
        return result.reshape(len(members), 2, LAT, NPC)

    def wait_for(blocks, sem):
        pltpu.make_async_copy(blocks, blocks, sem).wait()

    for k in range(PER):
        for first in range(0, MEM, PART):
            members = others[first : first + PART]
            block = shift_and_reduce(k, members)
            made[k, first : first + PART] = block
            for i, member in enumerate(members):
                if first + i == MEM - 1:
                    got[k, me] = block[i]
                else:
                    pltpu.make_async_remote_copy(
                        src_ref=made.at[k, first + i],
                        dst_ref=got.at[k, me],
                        send_sem=send_sem.at[k],
                        recv_sem=recv_sem.at[k],
                        device_id=(group, member),
                        device_id_type=MESH,
                    ).start()

    for k in range(PER):
        wait_for(got.at[k, pl.ds(0, MEM - 1)], recv_sem.at[k])
        h, l = halves(got[k].reshape(MEM * 2 * LAT, NPC))
        result = dot(theta_high[...], h) + dot(theta_low[...], h) + dot(theta_high[...], l)
        thin[k] = result.reshape(thin.shape[1:])
        for member in others[: MEM - 1]:
            pltpu.make_async_remote_copy(
                src_ref=thin.at[k, member],
                dst_ref=out.at[me * PER + k],
                send_sem=back_send.at[k],
                recv_sem=back_recv.at[k],
                device_id=(group, member),
                device_id_type=MESH,
            ).start()
        out[me * PER + k] = thin[k, me]

    for k in range(PER):
        wait_for(made.at[k, pl.ds(0, MEM - 1)], send_sem.at[k])
        wait_for(thin.at[k, pl.ds(0, MEM - 1)], back_send.at[k])
        wait_for(thin.at[k, pl.ds(0, MEM - 1)], back_recv.at[k])


def on_device(patterns, operators, partners, operator_index, child_parent, child_octant, *, constants):
    f32, bf16 = jnp.float32, jnp.bfloat16
    hbm = pl.BlockSpec(memory_space=pltpu.HBM)
    dma = pltpu.SemaphoreType.DMA
    return pl.pallas_call(
        kernel,
        out_shape=jax.ShapeDtypeStruct((CH, 2, OUT_LAT, NPC), f32),
        in_specs=[hbm] * (6 + len(constants)),
        out_specs=pl.BlockSpec(memory_space=pltpu.VMEM),
        scratch_shapes=[
            pltpu.SMEM((NPART, CL), jnp.int32),
            pltpu.SMEM((NPART, CL), jnp.int32),
            pltpu.SMEM((CH,), jnp.int32),
            pltpu.SMEM((CH,), jnp.int32),
            pltpu.VMEM((CL, 2, LAT, NP), f32),
            pltpu.VMEM((CL + 2 * BAND, 2, LAT, NP), f32),
            pltpu.VMEM(operators.shape, f32),
            pltpu.VMEM((2, LAT, NP), f32),
            pltpu.VMEM((2, LAT, 128), f32),
            pltpu.VMEM((NP, NPC), bf16),
            pltpu.VMEM((NP, NPC), bf16),
            pltpu.VMEM((2 * NTC, 2 * NT), bf16),
            pltpu.VMEM((2 * NTC, 2 * NT), bf16),
            pltpu.VMEM((8, 2, LAT, NP), f32),
            pltpu.VMEM((CL, 2, LAT, NP), f32),
            pltpu.VMEM((PART * 2 * LAT, NP), bf16),
            pltpu.VMEM((PART * 2 * LAT, NP), bf16),
            pltpu.VMEM((PER, MEM, 2, LAT, NPC), f32),
            pltpu.VMEM((PER, MEM, 2, LAT, NPC), f32),
            pltpu.VMEM((PER, MEM, 2, OUT_LAT, NPC), f32),
            dma((13,)),
            dma((2, HALO_PARTS)),
            dma((2, HALO_PARTS)),
            dma((PER,)),
            dma((PER,)),
            dma((PER,)),
            dma((PER,)),
            pltpu.SemaphoreType.REGULAR,
        ],
        compiler_params=pltpu.CompilerParams(
            collective_id=0, has_side_effects=True, vmem_limit_bytes=60 * 2**20
        ),
        cost_estimate=pl.CostEstimate(flops=10**9, bytes_accessed=6 * 2**20, transcendentals=0),
    )(partners.T, operator_index.T, child_parent, child_octant, patterns, operators, *constants)


def solution(mesh):
    constants = tables()
    whole = P("group", None, "member", None)
    return jax.shard_map(
        functools.partial(on_device, constants=constants),
        mesh=mesh,
        in_specs=(whole, P(None, None, "member", None), P("group", None), P("group", None), P("group"), P("group")),
        out_specs=whole,
        check_vma=False,
    )
```

```python
import functools

import jax
import jax.numpy as jnp
import ml_dtypes
import numpy as np
from jax import lax
from jax.experimental import pallas as pl
from jax.experimental.pallas import tpu as pltpu
from jax.sharding import PartitionSpec as P

MESH = pl.DeviceIdType.MESH

NT, NP, NTC, NPC = 256, 512, 128, 256
NPART = 8
CL = 32
CH = 64
BAND = 8
MEM = 32
LAT = NT // MEM
OUT_LAT = NTC // MEM
REACH = 6.0
HALO_PARTS = 1
FIRST = 16
CHIPS = 16
ROUNDS = ((0, 1), (1, 2), (2, 4))
PART = 8
STEPS = sorted(
    ((y, x) for y in range(4) for x in range(4)),
    key=lambda step: -min(step[0], 4 - step[0]) - min(step[1], 4 - step[1]),
)


def split(values):
    high = values.astype(ml_dtypes.bfloat16)
    low = (values - high.astype(np.float64)).astype(ml_dtypes.bfloat16)
    return high, low


def tables():
    theta_fine = np.pi * (np.arange(NT) + 0.5) / NT
    theta_coarse = np.pi * (np.arange(NTC) + 0.5) / NTC
    orders = np.arange(NTC)
    weights = np.where(orders > 0, 2.0, 1.0)
    theta = (np.cos(np.outer(theta_coarse, orders)) * weights) @ np.cos(np.outer(theta_fine, orders)).T / NT
    phi_fine = 2.0 * np.pi * np.arange(NP) / NP
    phi_coarse = 2.0 * np.pi * np.arange(NPC) / NPC
    modes = np.arange(NPC // 2 + 1)
    mode_weights = np.where((modes > 0) & (modes < NPC // 2), 2.0, 1.0)
    phi = (
        (np.cos(np.outer(phi_coarse, modes)) * mode_weights) @ np.cos(np.outer(phi_fine, modes)).T
        + (np.sin(np.outer(phi_coarse, modes)) * mode_weights) @ np.sin(np.outer(phi_fine, modes)).T
    ) / NP
    theta_high, theta_low = split(theta)
    phi_high, phi_low = split(phi.T)
    arg = REACH * np.sin(theta_fine)[:, None] * np.cos(phi_fine)[None, :]
    wave_x = np.stack([np.cos(arg), np.sin(arg)]).reshape(2, MEM, LAT, NP).swapaxes(0, 1)
    arg = np.broadcast_to(REACH * np.cos(theta_fine)[:, None], (NT, 128))
    wave_z = np.stack([np.cos(arg), np.sin(arg)]).reshape(2, MEM, LAT, 128).swapaxes(0, 1)
    return (
        wave_x.astype(np.float32),
        wave_z.astype(np.float32),
        phi_high,
        phi_low,
        theta_high,
        theta_low,
    )


def times(a, b):
    return a[0] * b[0] - a[1] * b[1], a[0] * b[1] + a[1] * b[0]


def halves(x):
    high = x.astype(jnp.bfloat16)
    return high, (x - high.astype(jnp.float32)).astype(jnp.bfloat16)


def dot(a, b):
    return jnp.dot(a, b, preferred_element_type=jnp.float32)


def kernel(
    partners_in, factors_in, parents_in, octants_in, patterns, operators, wave_x_in, wave_z_in, phi_high_in, phi_low_in, theta_high_in, theta_low_in,
    out, rank,
    partners, factors, parents, octants,
    own, wide, ops, wave_x, wave_z, phi_high, phi_low, theta_high, theta_low,
    order, order_held, phase, translated, high, low, made, got, thin,
    load_sem, halo_send, halo_recv, send_sem, recv_sem, back_send, back_recv, turn,
):
    group = lax.axis_index("group")
    me = lax.axis_index("member")
    groups = lax.axis_size("group")
    below, above = group - 1, group + 1
    has_below, has_above = group > 0, group < groups - 1

    def load(k, src, dst):
        return pltpu.make_async_copy(src, dst, load_sem.at[k])

    loads = [
        load(0, wave_x_in.at[me], wave_x),
        load(1, wave_z_in.at[me], wave_z),
        load(2, partners_in, partners),
        load(3, factors_in, factors),
        load(4, patterns, own),
        load(5, operators, ops),
        load(6, parents_in, parents),
        load(7, octants_in, octants),
        load(8, phi_high_in, phi_high),
        load(9, phi_low_in, phi_low),
        load(10, patterns, wide.at[pl.ds(BAND, CL)]),
        load(11, theta_high_in, theta_high),
        load(12, theta_low_in, theta_low),
    ]
    for one in loads:
        one.start()

    core = lax.rem(me, 2)
    ys = [lax.rem(me // 8 + step, 4) * 8 for step in range(4)]
    xs = [lax.rem(me // 2 + step, 4) * 2 for step in range(4)]
    chips = [ys[y] + xs[x] for y, x in STEPS]
    others = [chip + part for chip in chips[:-1] for part in range(2)] + [chips[-1] + 1 - core]

    barrier = pltpu.get_barrier_semaphore()

    @pl.when(has_above)
    def _():
        pl.semaphore_signal(barrier, inc=1, device_id=(above, me), device_id_type=MESH)

    @pl.when(has_below)
    def _():
        pl.semaphore_signal(barrier, inc=1, device_id=(below, me), device_id_type=MESH)

    for member in others:
        pl.semaphore_signal(barrier, inc=1, device_id=(group, member), device_id_type=MESH)

    for one in loads[:2]:
        one.wait()
    x_real, x_imag = wave_x[0], wave_x[1]

    def turned(v):
        return jnp.concatenate([v[:, NP - NP // 4 :], v[:, : NP - NP // 4]], axis=1)

    y_real, y_imag = turned(x_real), turned(x_imag)
    z_real = jnp.concatenate([wave_z[0]] * (NP // 128), axis=1)
    z_imag = jnp.concatenate([wave_z[1]] * (NP // 128), axis=1)
    for octant in range(8):
        sx, sy, sz = 1 - 2 * (octant % 2), 1 - 2 * (octant // 2 % 2), 1 - 2 * (octant // 4)
        xy = times((x_real, sx * x_imag), (y_real, sy * y_imag))
        full = times(xy, (z_real, sz * z_imag))
        phase[octant, 0], phase[octant, 1] = full

    def translate(cluster, cells, first):
        real = jnp.zeros((LAT, NP), jnp.float32)
        imag = jnp.zeros((LAT, NP), jnp.float32)
        for p in range(NPART):
            cell = cells[jnp.clip(partners[p, cluster] - first, 0, cells.shape[0] - 1)]
            factor = ops[factors[p, cluster]]
            part = times(factor, cell)
            real, imag = real + part[0], imag + part[1]
        translated[cluster, 0] = real
        translated[cluster, 1] = imag

    for one in loads[2:6]:
        one.wait()

    @pl.loop(BAND, CL - BAND)
    def _(cluster):
        translate(cluster, own, group * CL)

    for one in loads[6:10]:
        one.wait()
    inner = []
    for child in range(CH):
        row = lax.rem(parents[child], CL)
        inner.append(jnp.where((row >= BAND) & (row < CL - BAND), 1, 0))
    count = sum(inner)
    seen = jnp.int32(0)
    lane = lax.broadcasted_iota(jnp.int32, (8, 128), 1)
    child_of = jnp.zeros((8, 128), jnp.int32)
    for child in range(CH):
        place = jnp.where(inner[child] == 1, seen, count + child - seen)
        rank[child] = place
        child_of = jnp.where(lane == place, child, child_of)
        seen = seen + inner[child]
    order_held[...] = child_of
    ordering = pltpu.make_async_copy(order_held, order, load_sem.at[0])
    ordering.start()
    ordering.wait()

    def shift_and_reduce(begin, end, first, number):
        rounds = end - begin
        for n in range(number):
            for k in range(rounds):
                child = order[0, (begin + k) * FIRST + chips[first + n] // 2]
                parent = translated[lax.rem(parents[child], CL)]
                moved = times(parent, phase[octants[child]])
                h, l = halves(jnp.concatenate(moved, axis=0))
                at = (n * rounds + k) * 2 * LAT
                high[at : at + 2 * LAT, :] = h
                low[at : at + 2 * LAT, :] = l
        total = number * rounds * 2 * LAT
        h, l = high[:total, :], low[:total, :]
        result = dot(h, phi_high[...]) + dot(h, phi_low[...]) + dot(l, phi_high[...])
        result = result.reshape(number, rounds, 2, LAT, NPC)
        for n in range(number):
            made[begin:end, first + n] = result[n]

    def send(index, chip, part):
        begin, end = ROUNDS[index]
        pltpu.make_async_remote_copy(
            src_ref=made.at[pl.ds(begin, end - begin), chip, part],
            dst_ref=got.at[pl.ds(begin, end - begin), me],
            send_sem=send_sem.at[index],
            recv_sem=recv_sem.at[index],
            device_id=(group, chips[chip] + part),
            device_id_type=MESH,
        ).start()

    def send_chips(index, first, number):
        begin, end = ROUNDS[index]
        for chip in range(first, first + number):
            if chip < CHIPS - 1:
                send(index, chip, 0)
                send(index, chip, 1)
            else:
                send(index, chip, 1 - core)
                got[begin:end, me] = made[begin:end, chip, core]

    def wait_for(blocks, sem):
        pltpu.make_async_copy(blocks, blocks, sem).wait()

    for first in range(0, CHIPS, PART):
        shift_and_reduce(*ROUNDS[0], first, PART)

    pl.semaphore_wait(barrier, MEM - 1 + jnp.minimum(group, 1) + jnp.minimum(groups - 1 - group, 1))

    width = BAND // HALO_PARTS

    def up(n, to):
        return pltpu.make_async_remote_copy(
            src_ref=patterns.at[pl.ds(CL - BAND + n * width, width)],
            dst_ref=wide.at[pl.ds(n * width, width)],
            send_sem=halo_send.at[0, n],
            recv_sem=halo_recv.at[0, n],
            device_id=(to, me),
            device_id_type=MESH,
        )

    def down(n, to):
        return pltpu.make_async_remote_copy(
            src_ref=patterns.at[pl.ds(n * width, width)],
            dst_ref=wide.at[pl.ds(CL + BAND + n * width, width)],
            send_sem=halo_send.at[1, n],
            recv_sem=halo_recv.at[1, n],
            device_id=(to, me),
            device_id_type=MESH,
        )

    def start_halo():
        for n in range(HALO_PARTS):

            @pl.when(has_above)
            def _():
                up(n, above).start()

            @pl.when(has_below)
            def _():
                down(n, below).start()

    @pl.when(core == 0)
    def _():
        start_halo()

    send_chips(0, 0, CHIPS)

    @pl.when(core == 1)
    def _():
        pl.semaphore_wait(turn, 1)
        start_halo()

    for one in loads[10:]:
        one.wait()
    for n in range(HALO_PARTS):

        @pl.when(has_above)
        def _():
            up(n, above).wait_send()

        @pl.when(has_below)
        def _():
            down(n, below).wait_send()

    @pl.when(core == 0)
    def _():
        pl.semaphore_signal(turn, inc=1, device_id=(group, chips[-1] + 1), device_id_type=MESH)

    for n in range(HALO_PARTS):

        @pl.when(has_above)
        def _():
            down(n, above).wait_recv()

        @pl.when(has_below)
        def _():
            up(n, below).wait_recv()

    @pl.loop(0, 2 * BAND)
    def _(n):
        translate(jnp.where(n < BAND, n, n + CL - 2 * BAND), wide, group * CL - BAND)

    def mine(index):
        begin, end = ROUNDS[index]
        return pltpu.make_async_copy(
            thin.at[pl.ds(begin, end - begin), me],
            out.at[pl.ds(begin, end - begin), me // 2, core],
            load_sem.at[1 + index],
        )

    def finish(index):
        begin, end = ROUNDS[index]
        rounds = pl.ds(begin, end - begin)
        wait_for(got.at[rounds, pl.ds(0, MEM - 1)], recv_sem.at[index])
        for k in range(begin, end):
            h, l = halves(got[k].reshape(NT, NPC))
            result = dot(theta_high[...], h) + dot(theta_low[...], h) + dot(theta_high[...], l)
            thin[k] = result.reshape(MEM, OUT_LAT, NPC)
        for member in others:
            pltpu.make_async_remote_copy(
                src_ref=thin.at[rounds, member],
                dst_ref=out.at[rounds, me // 2, core],
                send_sem=back_send.at[index],
                recv_sem=back_recv.at[index],
                device_id=(group, member),
                device_id_type=MESH,
            ).start()
        mine(index).start()

    for index in range(1, len(ROUNDS)):
        begin, end = ROUNDS[index]
        number = PART // (end - begin)
        for first in range(0, CHIPS, number):
            shift_and_reduce(begin, end, first, number)
            send_chips(index, first, number)
        finish(index - 1)
    finish(len(ROUNDS) - 1)

    for index, (begin, end) in enumerate(ROUNDS):
        rounds = pl.ds(begin, end - begin)
        mine(index).wait()
        wait_for(got.at[rounds, pl.ds(0, MEM - 1)], send_sem.at[index])
        wait_for(thin.at[rounds, pl.ds(0, MEM - 1)], back_send.at[index])
        wait_for(thin.at[rounds, pl.ds(0, MEM - 1)], back_recv.at[index])


def reorder(rank, ranked, out, held, ordered, load_sem, store_sem):
    parts = 4
    number = CH // parts

    def load(part):
        rows = pl.ds(part * number, number)
        return pltpu.make_async_copy(ranked.at[rows], held.at[rows], load_sem.at[part])

    def store(part):
        rows = pl.ds(part * number, number)
        return pltpu.make_async_copy(ordered.at[rows], out.at[rows], store_sem.at[part])

    for part in range(parts):
        load(part).start()
    for part in range(parts):
        load(part).wait()
    for part in range(parts):
        for child in range(part * number, (part + 1) * number):
            ordered[child] = held[rank[child]]
        store(part).start()
    for part in range(parts):
        store(part).wait()


def on_device(patterns, operators, partners, operator_index, child_parent, child_octant, *, constants):
    f32, bf16 = jnp.float32, jnp.bfloat16
    hbm = pl.BlockSpec(memory_space=pltpu.HBM)
    dma = pltpu.SemaphoreType.DMA
    ranked, rank = pl.pallas_call(
        kernel,
        out_shape=(
            jax.ShapeDtypeStruct((CH // FIRST, CHIPS, 2, OUT_LAT, NPC), f32),
            jax.ShapeDtypeStruct((CH,), jnp.int32),
        ),
        in_specs=[hbm] * (6 + len(constants)),
        out_specs=(hbm, pl.BlockSpec(memory_space=pltpu.SMEM)),
        scratch_shapes=[
            pltpu.SMEM((NPART, CL), jnp.int32),
            pltpu.SMEM((NPART, CL), jnp.int32),
            pltpu.SMEM((CH,), jnp.int32),
            pltpu.SMEM((CH,), jnp.int32),
            pltpu.VMEM((CL, 2, LAT, NP), f32),
            pltpu.VMEM((CL + 2 * BAND, 2, LAT, NP), f32),
            pltpu.VMEM(operators.shape, f32),
            pltpu.VMEM((2, LAT, NP), f32),
            pltpu.VMEM((2, LAT, 128), f32),
            pltpu.VMEM((NP, NPC), bf16),
            pltpu.VMEM((NP, NPC), bf16),
            pltpu.VMEM((NTC, NT), bf16),
            pltpu.VMEM((NTC, NT), bf16),
            pltpu.SMEM((8, 128), jnp.int32),
            pltpu.VMEM((8, 128), jnp.int32),
            pltpu.VMEM((8, 2, LAT, NP), f32),
            pltpu.VMEM((CL, 2, LAT, NP), f32),
            pltpu.VMEM((PART * 2 * LAT, NP), bf16),
            pltpu.VMEM((PART * 2 * LAT, NP), bf16),
            pltpu.VMEM((CH // FIRST, CHIPS, 2, LAT, NPC), f32),
            pltpu.VMEM((CH // FIRST, MEM, LAT, NPC), f32),
            pltpu.VMEM((CH // FIRST, MEM, OUT_LAT, NPC), f32),
            dma((13,)),
            dma((2, HALO_PARTS)),
            dma((2, HALO_PARTS)),
            dma((len(ROUNDS),)),
            dma((len(ROUNDS),)),
            dma((len(ROUNDS),)),
            dma((len(ROUNDS),)),
            pltpu.SemaphoreType.REGULAR,
        ],
        compiler_params=pltpu.CompilerParams(
            collective_id=0, has_side_effects=True, vmem_limit_bytes=60 * 2**20
        ),
        cost_estimate=pl.CostEstimate(flops=10**9, bytes_accessed=6 * 2**20, transcendentals=0),
    )(partners.T, operator_index.T, child_parent, child_octant, patterns, operators, *constants)
    shape = (CH, 2, OUT_LAT, NPC)
    return pl.pallas_call(
        reorder,
        out_shape=jax.ShapeDtypeStruct(shape, f32),
        in_specs=[pl.BlockSpec(memory_space=pltpu.SMEM), hbm],
        out_specs=hbm,
        scratch_shapes=[pltpu.VMEM(shape, f32), pltpu.VMEM(shape, f32), dma((4,)), dma((4,))],
        compiler_params=pltpu.CompilerParams(vmem_limit_bytes=60 * 2**20),
    )(rank, ranked.reshape(shape))


def solution(mesh):
    constants = tables()
    whole = P("group", None, "member", None)
    return jax.shard_map(
        functools.partial(on_device, constants=constants),
        mesh=mesh,
        in_specs=(whole, P(None, None, "member", None), P("group", None), P("group", None), P("group"), P("group")),
        out_specs=whole,
        check_vma=False,
    )
```

```python
import functools

import jax
import jax.numpy as jnp
import ml_dtypes
import numpy as np
from jax import lax
from jax.experimental import pallas as pl
from jax.experimental.pallas import tpu as pltpu
from jax.sharding import PartitionSpec as P

MESH = pl.DeviceIdType.MESH

NT, NP, NTC, NPC = 256, 512, 128, 256
NPART = 8
CL = 32
CH = 64
BAND = 8
MEM = 32
LAT = NT // MEM
OUT_LAT = NTC // MEM
REACH = 6.0
HALO_PARTS = 1
FIRST = 16
CHIPS = 16
ROUNDS = ((0, 1), (1, 3), (3, 4))
PART = 8
STEPS = sorted(
    ((y, x) for y in range(4) for x in range(4)),
    key=lambda step: -min(step[0], 4 - step[0]) - min(step[1], 4 - step[1]),
)


def split(values):
    high = values.astype(ml_dtypes.bfloat16)
    low = (values - high.astype(np.float64)).astype(ml_dtypes.bfloat16)
    return high, low


def tables():
    theta_fine = np.pi * (np.arange(NT) + 0.5) / NT
    theta_coarse = np.pi * (np.arange(NTC) + 0.5) / NTC
    orders = np.arange(NTC)
    weights = np.where(orders > 0, 2.0, 1.0)
    theta = (np.cos(np.outer(theta_coarse, orders)) * weights) @ np.cos(np.outer(theta_fine, orders)).T / NT
    phi_fine = 2.0 * np.pi * np.arange(NP) / NP
    phi_coarse = 2.0 * np.pi * np.arange(NPC) / NPC
    modes = np.arange(NPC // 2 + 1)
    mode_weights = np.where((modes > 0) & (modes < NPC // 2), 2.0, 1.0)
    phi = (
        (np.cos(np.outer(phi_coarse, modes)) * mode_weights) @ np.cos(np.outer(phi_fine, modes)).T
        + (np.sin(np.outer(phi_coarse, modes)) * mode_weights) @ np.sin(np.outer(phi_fine, modes)).T
    ) / NP
    theta_high, theta_low = split(theta)
    phi_high, phi_low = split(phi.T)
    arg = REACH * np.sin(theta_fine)[:, None] * np.cos(phi_fine)[None, :]
    wave_x = np.stack([np.cos(arg), np.sin(arg)]).reshape(2, MEM, LAT, NP).swapaxes(0, 1)
    arg = np.broadcast_to(REACH * np.cos(theta_fine)[:, None], (NT, 128))
    wave_z = np.stack([np.cos(arg), np.sin(arg)]).reshape(2, MEM, LAT, 128).swapaxes(0, 1)
    return (
        wave_x.astype(np.float32),
        wave_z.astype(np.float32),
        phi_high,
        phi_low,
        theta_high,
        theta_low,
    )


def times(a, b):
    return a[0] * b[0] - a[1] * b[1], a[0] * b[1] + a[1] * b[0]


def halves(x):
    high = x.astype(jnp.bfloat16)
    return high, (x - high.astype(jnp.float32)).astype(jnp.bfloat16)


def dot(a, b):
    return jnp.dot(a, b, preferred_element_type=jnp.float32)


def kernel(
    partners_in, factors_in, parents_in, octants_in, patterns, operators, wave_x_in, wave_z_in, phi_high_in, phi_low_in, theta_high_in, theta_low_in,
    out, rank,
    partners, factors, parents, octants,
    own, wide, ops, wave_x, wave_z, phi_high, phi_low, theta_high, theta_low,
    order, order_held, phase, translated, high, low, made, got, thin,
    load_sem, halo_send, halo_recv, send_sem, recv_sem, back_send, back_recv, turn,
):
    group = lax.axis_index("group")
    me = lax.axis_index("member")
    groups = lax.axis_size("group")
    below, above = group - 1, group + 1
    has_below, has_above = group > 0, group < groups - 1

    def load(k, src, dst):
        return pltpu.make_async_copy(src, dst, load_sem.at[k])

    loads = [
        load(0, wave_x_in.at[me], wave_x),
        load(1, wave_z_in.at[me], wave_z),
        load(2, partners_in, partners),
        load(3, factors_in, factors),
        load(4, patterns, own),
        load(5, operators, ops),
        load(6, parents_in, parents),
        load(7, octants_in, octants),
        load(8, phi_high_in, phi_high),
        load(9, phi_low_in, phi_low),
        load(10, patterns, wide.at[pl.ds(BAND, CL)]),
        load(11, theta_high_in, theta_high),
        load(12, theta_low_in, theta_low),
    ]
    for one in loads:
        one.start()

    core = lax.rem(me, 2)
    ys = [lax.rem(me // 8 + step, 4) * 8 for step in range(4)]
    xs = [lax.rem(me // 2 + step, 4) * 2 for step in range(4)]
    chips = [ys[y] + xs[x] for y, x in STEPS]
    others = [chip + part for chip in chips[:-1] for part in range(2)] + [chips[-1] + 1 - core]

    barrier = pltpu.get_barrier_semaphore()

    @pl.when(has_above)
    def _():
        pl.semaphore_signal(barrier, inc=1, device_id=(above, me), device_id_type=MESH)

    @pl.when(has_below)
    def _():
        pl.semaphore_signal(barrier, inc=1, device_id=(below, me), device_id_type=MESH)

    for member in others:
        pl.semaphore_signal(barrier, inc=1, device_id=(group, member), device_id_type=MESH)

    for one in loads[:2]:
        one.wait()
    x_real, x_imag = wave_x[0], wave_x[1]

    def turned(v):
        return jnp.concatenate([v[:, NP - NP // 4 :], v[:, : NP - NP // 4]], axis=1)

    y_real, y_imag = turned(x_real), turned(x_imag)
    z_real = jnp.concatenate([wave_z[0]] * (NP // 128), axis=1)
    z_imag = jnp.concatenate([wave_z[1]] * (NP // 128), axis=1)
    for octant in range(8):
        sx, sy, sz = 1 - 2 * (octant % 2), 1 - 2 * (octant // 2 % 2), 1 - 2 * (octant // 4)
        xy = times((x_real, sx * x_imag), (y_real, sy * y_imag))
        full = times(xy, (z_real, sz * z_imag))
        phase[octant, 0], phase[octant, 1] = full

    pl.semaphore_wait(barrier, MEM - 1 + jnp.minimum(group, 1) + jnp.minimum(groups - 1 - group, 1))

    width = BAND // HALO_PARTS

    def up(n, to):
        return pltpu.make_async_remote_copy(
            src_ref=patterns.at[pl.ds(CL - BAND + n * width, width)],
            dst_ref=wide.at[pl.ds(n * width, width)],
            send_sem=halo_send.at[0, n],
            recv_sem=halo_recv.at[0, n],
            device_id=(to, me),
            device_id_type=MESH,
        )

    def down(n, to):
        return pltpu.make_async_remote_copy(
            src_ref=patterns.at[pl.ds(n * width, width)],
            dst_ref=wide.at[pl.ds(CL + BAND + n * width, width)],
            send_sem=halo_send.at[1, n],
            recv_sem=halo_recv.at[1, n],
            device_id=(to, me),
            device_id_type=MESH,
        )

    def start_halo():
        for n in range(HALO_PARTS):

            @pl.when(has_above)
            def _():
                up(n, above).start()

            @pl.when(has_below)
            def _():
                down(n, below).start()

    @pl.when(core == 0)
    def _():
        start_halo()

    def translate(cluster, cells, first):
        real = jnp.zeros((LAT, NP), jnp.float32)
        imag = jnp.zeros((LAT, NP), jnp.float32)
        for p in range(NPART):
            cell = cells[jnp.clip(partners[p, cluster] - first, 0, cells.shape[0] - 1)]
            factor = ops[factors[p, cluster]]
            part = times(factor, cell)
            real, imag = real + part[0], imag + part[1]
        translated[cluster, 0] = real
        translated[cluster, 1] = imag

    for one in loads[2:6]:
        one.wait()

    @pl.loop(BAND, CL - BAND)
    def _(cluster):
        translate(cluster, own, group * CL)

    def wait_sent():
        for n in range(HALO_PARTS):

            @pl.when(has_above)
            def _():
                up(n, above).wait_send()

            @pl.when(has_below)
            def _():
                down(n, below).wait_send()

    for one in loads[6:10]:
        one.wait()
    inner = []
    for child in range(CH):
        row = lax.rem(parents[child], CL)
        inner.append(jnp.where((row >= BAND) & (row < CL - BAND), 1, 0))
    count = sum(inner)
    seen = jnp.int32(0)
    lane = lax.broadcasted_iota(jnp.int32, (8, 128), 1)
    child_of = jnp.zeros((8, 128), jnp.int32)
    for child in range(CH):
        place = jnp.where(inner[child] == 1, seen, count + child - seen)
        rank[child] = place
        child_of = jnp.where(lane == place, child, child_of)
        seen = seen + inner[child]
    order_held[...] = child_of
    ordering = pltpu.make_async_copy(order_held, order, load_sem.at[0])
    ordering.start()
    ordering.wait()

    def shift_and_reduce(begin, end, first, number):
        rounds = end - begin
        for n in range(number):
            for k in range(rounds):
                child = order[0, (begin + k) * FIRST + chips[first + n] // 2]
                parent = translated[lax.rem(parents[child], CL)]
                moved = times(parent, phase[octants[child]])
                h, l = halves(jnp.concatenate(moved, axis=0))
                at = (n * rounds + k) * 2 * LAT
                high[at : at + 2 * LAT, :] = h
                low[at : at + 2 * LAT, :] = l
        total = number * rounds * 2 * LAT
        h, l = high[:total, :], low[:total, :]
        result = dot(h, phi_high[...]) + dot(h, phi_low[...]) + dot(l, phi_high[...])
        result = result.reshape(number, rounds, 2, LAT, NPC)
        for n in range(number):
            made[begin:end, first + n] = result[n]

    def send(index, chip, part):
        begin, end = ROUNDS[index]
        pltpu.make_async_remote_copy(
            src_ref=made.at[pl.ds(begin, end - begin), chip, part],
            dst_ref=got.at[pl.ds(begin, end - begin), me],
            send_sem=send_sem.at[index],
            recv_sem=recv_sem.at[index],
            device_id=(group, chips[chip] + part),
            device_id_type=MESH,
        ).start()

    def send_chips(index, first, number):
        begin, end = ROUNDS[index]
        for chip in range(first, first + number):
            if chip < CHIPS - 1:
                send(index, chip, 0)
                send(index, chip, 1)
            else:
                send(index, chip, 1 - core)
                got[begin:end, me] = made[begin:end, chip, core]

    def wait_for(blocks, sem):
        pltpu.make_async_copy(blocks, blocks, sem).wait()

    for first in range(0, CHIPS, PART):
        shift_and_reduce(*ROUNDS[0], first, PART)

    send_chips(0, 0, CHIPS)

    @pl.when(core == 0)
    def _():
        wait_sent()
        pl.semaphore_signal(turn, inc=1, device_id=(group, chips[-1] + 1), device_id_type=MESH)

    @pl.when(core == 1)
    def _():
        pl.semaphore_wait(turn, 1)
        start_halo()

    for one in loads[10:]:
        one.wait()

    def mine(index):
        begin, end = ROUNDS[index]
        return pltpu.make_async_copy(
            thin.at[pl.ds(begin, end - begin), me],
            out.at[pl.ds(begin, end - begin), me // 2, core],
            load_sem.at[1 + index],
        )

    def finish(index):
        begin, end = ROUNDS[index]
        rounds = pl.ds(begin, end - begin)
        wait_for(got.at[rounds, pl.ds(0, MEM - 1)], recv_sem.at[index])
        for k in range(begin, end):
            h, l = halves(got[k].reshape(NT, NPC))
            result = dot(theta_high[...], h) + dot(theta_low[...], h) + dot(theta_high[...], l)
            thin[k] = result.reshape(MEM, OUT_LAT, NPC)
        for member in others:
            pltpu.make_async_remote_copy(
                src_ref=thin.at[rounds, member],
                dst_ref=out.at[rounds, me // 2, core],
                send_sem=back_send.at[index],
                recv_sem=back_recv.at[index],
                device_id=(group, member),
                device_id_type=MESH,
            ).start()
        mine(index).start()

    @pl.when(core == 1)
    def _():
        finish(0)

    for n in range(HALO_PARTS):

        @pl.when(has_above)
        def _():
            down(n, above).wait_recv()

        @pl.when(has_below)
        def _():
            up(n, below).wait_recv()

    @pl.loop(0, 2 * BAND)
    def _(n):
        translate(jnp.where(n < BAND, n, n + CL - 2 * BAND), wide, group * CL - BAND)

    for index in range(1, len(ROUNDS)):
        begin, end = ROUNDS[index]
        number = PART // (end - begin)
        for first in range(0, CHIPS, number):
            shift_and_reduce(begin, end, first, number)
            send_chips(index, first, number)
        if index == 1:

            @pl.when(core == 0)
            def _():
                finish(0)

        else:
            finish(index - 1)
    finish(len(ROUNDS) - 1)

    @pl.when(core == 1)
    def _():
        wait_sent()

    for index, (begin, end) in enumerate(ROUNDS):
        rounds = pl.ds(begin, end - begin)
        mine(index).wait()
        wait_for(got.at[rounds, pl.ds(0, MEM - 1)], send_sem.at[index])
        wait_for(thin.at[rounds, pl.ds(0, MEM - 1)], back_send.at[index])
        wait_for(thin.at[rounds, pl.ds(0, MEM - 1)], back_recv.at[index])


def reorder(rank_in, ranked, out, rank, held, ordered, load_sem, store_sem):
    parts = 4
    number = CH // parts

    def load(part):
        rows = pl.ds(part * number, number)
        return pltpu.make_async_copy(ranked.at[rows], held.at[rows], load_sem.at[part])

    def store(part):
        rows = pl.ds(part * number, number)
        return pltpu.make_async_copy(ordered.at[rows], out.at[rows], store_sem.at[part])

    ranks = pltpu.make_async_copy(rank_in, rank, load_sem.at[parts])
    ranks.start()
    for part in range(parts):
        load(part).start()
    ranks.wait()
    for part in range(parts):
        load(part).wait()
    for part in range(parts):
        for child in range(part * number, (part + 1) * number):
            ordered[child] = held[rank[child]]
        store(part).start()
    for part in range(parts):
        store(part).wait()


def on_device(patterns, operators, partners, operator_index, child_parent, child_octant, *, constants):
    f32, bf16 = jnp.float32, jnp.bfloat16
    hbm = pl.BlockSpec(memory_space=pltpu.HBM)
    dma = pltpu.SemaphoreType.DMA
    ranked, rank = pl.pallas_call(
        kernel,
        out_shape=(
            jax.ShapeDtypeStruct((CH // FIRST, CHIPS, 2, OUT_LAT, NPC), f32),
            jax.ShapeDtypeStruct((CH,), jnp.int32),
        ),
        in_specs=[hbm] * (6 + len(constants)),
        out_specs=(hbm, pl.BlockSpec(memory_space=pltpu.SMEM)),
        scratch_shapes=[
            pltpu.SMEM((NPART, CL), jnp.int32),
            pltpu.SMEM((NPART, CL), jnp.int32),
            pltpu.SMEM((CH,), jnp.int32),
            pltpu.SMEM((CH,), jnp.int32),
            pltpu.VMEM((CL, 2, LAT, NP), f32),
            pltpu.VMEM((CL + 2 * BAND, 2, LAT, NP), f32),
            pltpu.VMEM(operators.shape, f32),
            pltpu.VMEM((2, LAT, NP), f32),
            pltpu.VMEM((2, LAT, 128), f32),
            pltpu.VMEM((NP, NPC), bf16),
            pltpu.VMEM((NP, NPC), bf16),
            pltpu.VMEM((NTC, NT), bf16),
            pltpu.VMEM((NTC, NT), bf16),
            pltpu.SMEM((8, 128), jnp.int32),
            pltpu.VMEM((8, 128), jnp.int32),
            pltpu.VMEM((8, 2, LAT, NP), f32),
            pltpu.VMEM((CL, 2, LAT, NP), f32),
            pltpu.VMEM((PART * 2 * LAT, NP), bf16),
            pltpu.VMEM((PART * 2 * LAT, NP), bf16),
            pltpu.VMEM((CH // FIRST, CHIPS, 2, LAT, NPC), f32),
            pltpu.VMEM((CH // FIRST, MEM, LAT, NPC), f32),
            pltpu.VMEM((CH // FIRST, MEM, OUT_LAT, NPC), f32),
            dma((13,)),
            dma((2, HALO_PARTS)),
            dma((2, HALO_PARTS)),
            dma((len(ROUNDS),)),
            dma((len(ROUNDS),)),
            dma((len(ROUNDS),)),
            dma((len(ROUNDS),)),
            pltpu.SemaphoreType.REGULAR,
        ],
        compiler_params=pltpu.CompilerParams(
            collective_id=0, has_side_effects=True, vmem_limit_bytes=60 * 2**20
        ),
        cost_estimate=pl.CostEstimate(flops=10**9, bytes_accessed=6 * 2**20, transcendentals=0),
    )(partners.T, operator_index.T, child_parent, child_octant, patterns, operators, *constants)
    shape = (CH, 2, OUT_LAT, NPC)
    return pl.pallas_call(
        reorder,
        out_shape=jax.ShapeDtypeStruct(shape, f32),
        in_specs=[hbm, hbm],
        out_specs=hbm,
        scratch_shapes=[pltpu.SMEM((CH,), jnp.int32), pltpu.VMEM(shape, f32), pltpu.VMEM(shape, f32), dma((5,)), dma((4,))],
        compiler_params=pltpu.CompilerParams(vmem_limit_bytes=60 * 2**20),
    )(rank, ranked.reshape(shape))


def solution(mesh):
    constants = tables()
    whole = P("group", None, "member", None)
    return jax.shard_map(
        functools.partial(on_device, constants=constants),
        mesh=mesh,
        in_specs=(whole, P(None, None, "member", None), P("group", None), P("group", None), P("group"), P("group")),
        out_specs=whole,
        check_vma=False,
    )
```

```python
import functools

import jax
import jax.numpy as jnp
import ml_dtypes
import numpy as np
from jax import lax
from jax.experimental import pallas as pl
from jax.experimental.pallas import tpu as pltpu
from jax.sharding import PartitionSpec as P

MESH = pl.DeviceIdType.MESH

NT, NP, NTC, NPC = 256, 512, 128, 256
NPART = 8
CL = 32
CH = 64
BAND = 8
MEM = 32
LAT = NT // MEM
OUT_LAT = NTC // MEM
REACH = 6.0
HALO_PARTS = 1
FIRST = 16
CHIPS = 16
ROUNDS = ((0, 1), (1, 3), (3, 4))
PART = 8
STEPS = sorted(
    ((y, x) for y in range(4) for x in range(4)),
    key=lambda step: -min(step[0], 4 - step[0]) - min(step[1], 4 - step[1]),
)


def split(values):
    high = values.astype(ml_dtypes.bfloat16)
    low = (values - high.astype(np.float64)).astype(ml_dtypes.bfloat16)
    return high, low


def tables():
    theta_fine = np.pi * (np.arange(NT) + 0.5) / NT
    theta_coarse = np.pi * (np.arange(NTC) + 0.5) / NTC
    orders = np.arange(NTC)
    weights = np.where(orders > 0, 2.0, 1.0)
    theta = (np.cos(np.outer(theta_coarse, orders)) * weights) @ np.cos(np.outer(theta_fine, orders)).T / NT
    phi_fine = 2.0 * np.pi * np.arange(NP) / NP
    phi_coarse = 2.0 * np.pi * np.arange(NPC) / NPC
    modes = np.arange(NPC // 2 + 1)
    mode_weights = np.where((modes > 0) & (modes < NPC // 2), 2.0, 1.0)
    phi = (
        (np.cos(np.outer(phi_coarse, modes)) * mode_weights) @ np.cos(np.outer(phi_fine, modes)).T
        + (np.sin(np.outer(phi_coarse, modes)) * mode_weights) @ np.sin(np.outer(phi_fine, modes)).T
    ) / NP
    theta_high, theta_low = split(theta)
    phi_high, phi_low = split(phi.T)
    arg = REACH * np.sin(theta_fine)[:, None] * np.cos(phi_fine)[None, :]
    wave_x = np.stack([np.cos(arg), np.sin(arg)]).reshape(2, MEM, LAT, NP).swapaxes(0, 1)
    arg = np.broadcast_to(REACH * np.cos(theta_fine)[:, None], (NT, 128))
    wave_z = np.stack([np.cos(arg), np.sin(arg)]).reshape(2, MEM, LAT, 128).swapaxes(0, 1)
    return (
        wave_x.astype(np.float32),
        wave_z.astype(np.float32),
        phi_high,
        phi_low,
        theta_high,
        theta_low,
    )


def times(a, b):
    return a[0] * b[0] - a[1] * b[1], a[0] * b[1] + a[1] * b[0]


def halves(x):
    high = x.astype(jnp.bfloat16)
    return high, (x - high.astype(jnp.float32)).astype(jnp.bfloat16)


def dot(a, b):
    return jnp.dot(a, b, preferred_element_type=jnp.float32)


def kernel(
    partners_in, factors_in, parents_in, octants_in, patterns, operators, wave_x_in, wave_z_in, phi_high_in, phi_low_in, theta_high_in, theta_low_in,
    out, rank,
    partners, factors, parents, octants,
    own, wide, ops, wave_x, wave_z, phi_high, phi_low, theta_high, theta_low,
    order, order_held, phase, translated, high, low, made, got, thin,
    load_sem, halo_send, halo_recv, send_sem, recv_sem, back_send, back_recv, turn,
):
    group = lax.axis_index("group")
    me = lax.axis_index("member")
    groups = lax.axis_size("group")
    below, above = group - 1, group + 1
    has_below, has_above = group > 0, group < groups - 1

    def load(k, src, dst):
        return pltpu.make_async_copy(src, dst, load_sem.at[k])

    loads = [
        load(0, wave_x_in.at[me], wave_x),
        load(1, wave_z_in.at[me], wave_z),
        load(2, partners_in, partners),
        load(3, factors_in, factors),
        load(4, patterns, own),
        load(5, operators, ops),
        load(6, parents_in, parents),
        load(7, octants_in, octants),
        load(8, phi_high_in, phi_high),
        load(9, phi_low_in, phi_low),
        load(10, patterns, wide.at[pl.ds(BAND, CL)]),
        load(11, theta_high_in, theta_high),
        load(12, theta_low_in, theta_low),
    ]
    for one in loads:
        one.start()

    core = lax.rem(me, 2)
    ys = [lax.rem(me // 8 + step, 4) * 8 for step in range(4)]
    xs = [lax.rem(me // 2 + step, 4) * 2 for step in range(4)]
    chips = [ys[y] + xs[x] for y, x in STEPS]
    others = [chip + part for chip in chips[:-1] for part in range(2)] + [chips[-1] + 1 - core]

    barrier = pltpu.get_barrier_semaphore()

    @pl.when(has_above)
    def _():
        pl.semaphore_signal(barrier, inc=1, device_id=(above, me), device_id_type=MESH)

    @pl.when(has_below)
    def _():
        pl.semaphore_signal(barrier, inc=1, device_id=(below, me), device_id_type=MESH)

    for member in others:
        pl.semaphore_signal(barrier, inc=1, device_id=(group, member), device_id_type=MESH)

    for one in loads[:2]:
        one.wait()
    x_real, x_imag = wave_x[0], wave_x[1]

    def turned(v):
        return jnp.concatenate([v[:, NP - NP // 4 :], v[:, : NP - NP // 4]], axis=1)

    y_real, y_imag = turned(x_real), turned(x_imag)
    z_real = jnp.concatenate([wave_z[0]] * (NP // 128), axis=1)
    z_imag = jnp.concatenate([wave_z[1]] * (NP // 128), axis=1)
    for octant in range(8):
        sx, sy, sz = 1 - 2 * (octant % 2), 1 - 2 * (octant // 2 % 2), 1 - 2 * (octant // 4)
        xy = times((x_real, sx * x_imag), (y_real, sy * y_imag))
        full = times(xy, (z_real, sz * z_imag))
        phase[octant, 0], phase[octant, 1] = full

    pl.semaphore_wait(barrier, MEM - 1 + jnp.minimum(group, 1) + jnp.minimum(groups - 1 - group, 1))

    width = BAND // HALO_PARTS

    def up(n, to):
        return pltpu.make_async_remote_copy(
            src_ref=patterns.at[pl.ds(CL - BAND + n * width, width)],
            dst_ref=wide.at[pl.ds(n * width, width)],
            send_sem=halo_send.at[0, n],
            recv_sem=halo_recv.at[0, n],
            device_id=(to, me),
            device_id_type=MESH,
        )

    def down(n, to):
        return pltpu.make_async_remote_copy(
            src_ref=patterns.at[pl.ds(n * width, width)],
            dst_ref=wide.at[pl.ds(CL + BAND + n * width, width)],
            send_sem=halo_send.at[1, n],
            recv_sem=halo_recv.at[1, n],
            device_id=(to, me),
            device_id_type=MESH,
        )

    def start_halo():
        for n in range(HALO_PARTS):

            @pl.when(has_above)
            def _():
                up(n, above).start()

            @pl.when(has_below)
            def _():
                down(n, below).start()

    @pl.when(core == 0)
    def _():
        start_halo()

    def translate(cluster, cells, first):
        real = jnp.zeros((LAT, NP), jnp.float32)
        imag = jnp.zeros((LAT, NP), jnp.float32)
        for p in range(NPART):
            cell = cells[jnp.clip(partners[p, cluster] - first, 0, cells.shape[0] - 1)]
            factor = ops[factors[p, cluster]]
            part = times(factor, cell)
            real, imag = real + part[0], imag + part[1]
        translated[cluster, 0] = real
        translated[cluster, 1] = imag

    for one in loads[2:6]:
        one.wait()

    @pl.loop(BAND, CL - BAND)
    def _(cluster):
        translate(cluster, own, group * CL)

    def wait_sent():
        for n in range(HALO_PARTS):

            @pl.when(has_above)
            def _():
                up(n, above).wait_send()

            @pl.when(has_below)
            def _():
                down(n, below).wait_send()

    for one in loads[6:10]:
        one.wait()
    inner = []
    for child in range(CH):
        row = lax.rem(parents[child], CL)
        inner.append(jnp.where((row >= BAND) & (row < CL - BAND), 1, 0))
    count = sum(inner)
    seen = jnp.int32(0)
    lane = lax.broadcasted_iota(jnp.int32, (8, 128), 1)
    child_of = jnp.zeros((8, 128), jnp.int32)
    for child in range(CH):
        place = jnp.where(inner[child] == 1, seen, count + child - seen)
        rank[child] = place
        child_of = jnp.where(lane == place, child, child_of)
        seen = seen + inner[child]
    order_held[...] = child_of
    ordering = pltpu.make_async_copy(order_held, order, load_sem.at[0])
    ordering.start()
    ordering.wait()

    def shift_and_reduce(begin, end, first, number):
        rounds = end - begin
        for n in range(number):
            for k in range(rounds):
                child = order[0, (begin + k) * FIRST + chips[first + n] // 2]
                parent = translated[lax.rem(parents[child], CL)]
                moved = times(parent, phase[octants[child]])
                h, l = halves(jnp.concatenate(moved, axis=0))
                at = (n * rounds + k) * 2 * LAT
                high[at : at + 2 * LAT, :] = h
                low[at : at + 2 * LAT, :] = l
        total = number * rounds * 2 * LAT
        h, l = high[:total, :], low[:total, :]
        result = dot(h, phi_high[...]) + dot(h, phi_low[...]) + dot(l, phi_high[...])
        result = result.reshape(number, rounds, 2, LAT, NPC)
        for n in range(number):
            made[begin:end, first + n] = result[n]

    def send(index, chip, part):
        begin, end = ROUNDS[index]
        pltpu.make_async_remote_copy(
            src_ref=made.at[pl.ds(begin, end - begin), chip, part],
            dst_ref=got.at[pl.ds(begin, end - begin), me],
            send_sem=send_sem.at[index],
            recv_sem=recv_sem.at[index],
            device_id=(group, chips[chip] + part),
            device_id_type=MESH,
        ).start()

    def send_chips(index, first, number):
        begin, end = ROUNDS[index]
        for chip in range(first, first + number):
            if chip < CHIPS - 1:
                send(index, chip, 0)
                send(index, chip, 1)
            else:
                send(index, chip, 1 - core)
                got[begin:end, me] = made[begin:end, chip, core]

    def wait_for(blocks, sem):
        pltpu.make_async_copy(blocks, blocks, sem).wait()

    for first in range(0, CHIPS, PART):
        shift_and_reduce(*ROUNDS[0], first, PART)

    send_chips(0, 0, CHIPS)

    @pl.when(core == 0)
    def _():
        wait_sent()
        pl.semaphore_signal(turn, inc=1, device_id=(group, chips[-1] + 1), device_id_type=MESH)

    @pl.when(core == 1)
    def _():
        pl.semaphore_wait(turn, 1)
        start_halo()

    for one in loads[10:]:
        one.wait()

    def mine(index):
        begin, end = ROUNDS[index]
        return pltpu.make_async_copy(
            thin.at[pl.ds(begin, end - begin), me],
            out.at[pl.ds(begin, end - begin), me // 2, core],
            load_sem.at[1 + index],
        )

    def finish(index):
        begin, end = ROUNDS[index]
        rounds = pl.ds(begin, end - begin)
        wait_for(got.at[rounds, pl.ds(0, MEM - 1)], recv_sem.at[index])
        for k in range(begin, end):
            h, l = halves(got[k].reshape(NT, NPC))
            result = dot(theta_high[...], h) + dot(theta_low[...], h) + dot(theta_high[...], l)
            thin[k] = result.reshape(MEM, OUT_LAT, NPC)
        for member in others:
            pltpu.make_async_remote_copy(
                src_ref=thin.at[rounds, member],
                dst_ref=out.at[rounds, me // 2, core],
                send_sem=back_send.at[index],
                recv_sem=back_recv.at[index],
                device_id=(group, member),
                device_id_type=MESH,
            ).start()
        mine(index).start()

    @pl.when(core == 1)
    def _():
        finish(0)

    for n in range(HALO_PARTS):

        @pl.when(has_above)
        def _():
            down(n, above).wait_recv()

        @pl.when(has_below)
        def _():
            up(n, below).wait_recv()

    @pl.loop(0, 2 * BAND)
    def _(n):
        translate(jnp.where(n < BAND, n, n + CL - 2 * BAND), wide, group * CL - BAND)

    for index in range(1, len(ROUNDS)):
        begin, end = ROUNDS[index]
        number = PART // (end - begin)
        for first in range(0, CHIPS, number):
            shift_and_reduce(begin, end, first, number)
            send_chips(index, first, number)
        if index == 1:

            @pl.when(core == 0)
            def _():
                finish(0)

        else:
            finish(index - 1)
    finish(len(ROUNDS) - 1)

    @pl.when(core == 1)
    def _():
        wait_sent()

    for index, (begin, end) in enumerate(ROUNDS):
        rounds = pl.ds(begin, end - begin)
        mine(index).wait()
        wait_for(got.at[rounds, pl.ds(0, MEM - 1)], send_sem.at[index])
        wait_for(thin.at[rounds, pl.ds(0, MEM - 1)], back_send.at[index])
        wait_for(thin.at[rounds, pl.ds(0, MEM - 1)], back_recv.at[index])


def reorder(rank_in, ranked, out, rank, ordered, load_sem, store_sem):
    ranks = pltpu.make_async_copy(rank_in, rank, load_sem)
    ranks.start()
    parts = 4
    number = CH // parts

    def store(part):
        rows = pl.ds(part * number, number)
        return pltpu.make_async_copy(ordered.at[rows], out.at[rows], store_sem.at[part])

    ranks.wait()
    for part in range(parts):
        for child in range(part * number, (part + 1) * number):
            ordered[child] = ranked[rank[child]]
        store(part).start()
    for part in range(parts):
        store(part).wait()


def on_device(patterns, operators, partners, operator_index, child_parent, child_octant, *, constants):
    f32, bf16 = jnp.float32, jnp.bfloat16
    hbm = pl.BlockSpec(memory_space=pltpu.HBM)
    dma = pltpu.SemaphoreType.DMA
    operands = (partners.T, operator_index.T, child_parent, child_octant, patterns, operators, *constants)
    ranked, rank = pl.pallas_call(
        kernel,
        out_shape=(
            pltpu.VMEM((CH // FIRST, CHIPS, 2, OUT_LAT, NPC), f32),
            jax.ShapeDtypeStruct((CH,), jnp.int32),
        ),
        in_specs=[hbm] * (6 + len(constants)),
        out_specs=(pl.BlockSpec(memory_space=pltpu.VMEM), pl.BlockSpec(memory_space=pltpu.SMEM)),
        scratch_shapes=[
            pltpu.SMEM((NPART, CL), jnp.int32),
            pltpu.SMEM((NPART, CL), jnp.int32),
            pltpu.SMEM((CH,), jnp.int32),
            pltpu.SMEM((CH,), jnp.int32),
            pltpu.VMEM((CL, 2, LAT, NP), f32),
            pltpu.VMEM((CL + 2 * BAND, 2, LAT, NP), f32),
            pltpu.VMEM(operators.shape, f32),
            pltpu.VMEM((2, LAT, NP), f32),
            pltpu.VMEM((2, LAT, 128), f32),
            pltpu.VMEM((NP, NPC), bf16),
            pltpu.VMEM((NP, NPC), bf16),
            pltpu.VMEM((NTC, NT), bf16),
            pltpu.VMEM((NTC, NT), bf16),
            pltpu.SMEM((8, 128), jnp.int32),
            pltpu.VMEM((8, 128), jnp.int32),
            pltpu.VMEM((8, 2, LAT, NP), f32),
            pltpu.VMEM((CL, 2, LAT, NP), f32),
            pltpu.VMEM((PART * 2 * LAT, NP), bf16),
            pltpu.VMEM((PART * 2 * LAT, NP), bf16),
            pltpu.VMEM((CH // FIRST, CHIPS, 2, LAT, NPC), f32),
            pltpu.VMEM((CH // FIRST, MEM, LAT, NPC), f32),
            pltpu.VMEM((CH // FIRST, MEM, OUT_LAT, NPC), f32),
            dma((13,)),
            dma((2, HALO_PARTS)),
            dma((2, HALO_PARTS)),
            dma((len(ROUNDS),)),
            dma((len(ROUNDS),)),
            dma((len(ROUNDS),)),
            dma((len(ROUNDS),)),
            pltpu.SemaphoreType.REGULAR,
        ],
        compiler_params=pltpu.CompilerParams(
            collective_id=0, has_side_effects=True, vmem_limit_bytes=40 * 2**20
        ),
        cost_estimate=pl.CostEstimate(flops=10**9, bytes_accessed=6 * 2**20, transcendentals=0),
    )(*(pltpu.with_memory_space_constraint(jnp.asarray(x), pltpu.HBM) for x in operands))
    shape = (CH, 2, OUT_LAT, NPC)
    return pl.pallas_call(
        reorder,
        out_shape=jax.ShapeDtypeStruct(shape, f32),
        in_specs=[hbm, pl.BlockSpec(memory_space=pltpu.VMEM)],
        out_specs=hbm,
        scratch_shapes=[pltpu.SMEM((CH,), jnp.int32), pltpu.VMEM(shape, f32), dma(()), dma((4,))],
        compiler_params=pltpu.CompilerParams(vmem_limit_bytes=40 * 2**20),
    )(rank, ranked.reshape(shape))


def solution(mesh):
    constants = tables()
    whole = P("group", None, "member", None)
    return jax.shard_map(
        functools.partial(on_device, constants=constants),
        mesh=mesh,
        in_specs=(whole, P(None, None, "member", None), P("group", None), P("group", None), P("group"), P("group")),
        out_specs=whole,
        check_vma=False,
    )
```

```python
import functools

import jax
import jax.numpy as jnp
import ml_dtypes
import numpy as np
from jax import lax
from jax.experimental import pallas as pl
from jax.experimental.pallas import tpu as pltpu
from jax.sharding import PartitionSpec as P

MESH = pl.DeviceIdType.MESH

NT, NP, NTC, NPC = 256, 512, 128, 256
NPART = 8
CL = 32
CH = 64
BAND = 8
MEM = 32
LAT = NT // MEM
OUT_LAT = NTC // MEM
REACH = 6.0
HALO_PARTS = 1
FIRST = 16
CHIPS = 16
ROUNDS = ((0, 1), (1, 2), (2, 3), (3, 4))
PART = 8
STEPS = sorted(
    ((y, x) for y in range(4) for x in range(4)),
    key=lambda step: -min(step[0], 4 - step[0]) - min(step[1], 4 - step[1]),
)


def split(values):
    high = values.astype(ml_dtypes.bfloat16)
    low = (values - high.astype(np.float64)).astype(ml_dtypes.bfloat16)
    return high, low


def tables():
    theta_fine = np.pi * (np.arange(NT) + 0.5) / NT
    theta_coarse = np.pi * (np.arange(NTC) + 0.5) / NTC
    orders = np.arange(NTC)
    weights = np.where(orders > 0, 2.0, 1.0)
    theta = (np.cos(np.outer(theta_coarse, orders)) * weights) @ np.cos(np.outer(theta_fine, orders)).T / NT
    phi_fine = 2.0 * np.pi * np.arange(NP) / NP
    phi_coarse = 2.0 * np.pi * np.arange(NPC) / NPC
    modes = np.arange(NPC // 2 + 1)
    mode_weights = np.where((modes > 0) & (modes < NPC // 2), 2.0, 1.0)
    phi = (
        (np.cos(np.outer(phi_coarse, modes)) * mode_weights) @ np.cos(np.outer(phi_fine, modes)).T
        + (np.sin(np.outer(phi_coarse, modes)) * mode_weights) @ np.sin(np.outer(phi_fine, modes)).T
    ) / NP
    theta_high, theta_low = split(theta)
    phi_high, phi_low = split(phi.T)
    arg = REACH * np.sin(theta_fine)[:, None] * np.cos(phi_fine)[None, :]
    wave_x = np.stack([np.cos(arg), np.sin(arg)]).reshape(2, MEM, LAT, NP).swapaxes(0, 1)
    arg = np.broadcast_to(REACH * np.cos(theta_fine)[:, None], (NT, 128))
    wave_z = np.stack([np.cos(arg), np.sin(arg)]).reshape(2, MEM, LAT, 128).swapaxes(0, 1)
    return (
        wave_x.astype(np.float32),
        wave_z.astype(np.float32),
        phi_high,
        phi_low,
        theta_high,
        theta_low,
    )


def times(a, b):
    return a[0] * b[0] - a[1] * b[1], a[0] * b[1] + a[1] * b[0]


def halves(x):
    high = x.astype(jnp.bfloat16)
    return high, (x - high.astype(jnp.float32)).astype(jnp.bfloat16)


def dot(a, b):
    return jnp.dot(a, b, preferred_element_type=jnp.float32)


def kernel(
    partners_in, factors_in, parents_in, octants_in, patterns, operators, wave_x_in, wave_z_in, phi_high_in, phi_low_in, theta_high_in, theta_low_in,
    out, rank,
    partners, factors, parents, octants,
    own, wide, ops, wave_x, wave_z, phi_high, phi_low, theta_high, theta_low,
    order, order_held, phase, translated, high, low, made, got, thin,
    load_sem, halo_send, halo_recv, send_sem, recv_sem, back_send, back_recv, turn,
):
    group = lax.axis_index("group")
    me = lax.axis_index("member")
    groups = lax.axis_size("group")
    below, above = group - 1, group + 1
    has_below, has_above = group > 0, group < groups - 1

    def load(k, src, dst):
        return pltpu.make_async_copy(src, dst, load_sem.at[k])

    loads = [
        load(0, wave_x_in.at[me], wave_x),
        load(1, wave_z_in.at[me], wave_z),
        load(2, partners_in, partners),
        load(3, factors_in, factors),
        load(4, patterns, own),
        load(5, operators, ops),
        load(6, parents_in, parents),
        load(7, octants_in, octants),
        load(8, phi_high_in, phi_high),
        load(9, phi_low_in, phi_low),
        load(10, patterns, wide.at[pl.ds(BAND, CL)]),
        load(11, theta_high_in, theta_high),
        load(12, theta_low_in, theta_low),
    ]
    for one in loads:
        one.start()

    core = lax.rem(me, 2)
    ys = [lax.rem(me // 8 + step, 4) * 8 for step in range(4)]
    xs = [lax.rem(me // 2 + step, 4) * 2 for step in range(4)]
    chips = [ys[y] + xs[x] for y, x in STEPS]
    others = [chip + part for chip in chips[:-1] for part in range(2)] + [chips[-1] + 1 - core]

    barrier = pltpu.get_barrier_semaphore()

    @pl.when(has_above)
    def _():
        pl.semaphore_signal(barrier, inc=1, device_id=(above, me), device_id_type=MESH)

    @pl.when(has_below)
    def _():
        pl.semaphore_signal(barrier, inc=1, device_id=(below, me), device_id_type=MESH)

    for member in others:
        pl.semaphore_signal(barrier, inc=1, device_id=(group, member), device_id_type=MESH)

    for one in loads[:2]:
        one.wait()
    x_real, x_imag = wave_x[0], wave_x[1]

    def turned(v):
        return jnp.concatenate([v[:, NP - NP // 4 :], v[:, : NP - NP // 4]], axis=1)

    y_real, y_imag = turned(x_real), turned(x_imag)
    z_real = jnp.concatenate([wave_z[0]] * (NP // 128), axis=1)
    z_imag = jnp.concatenate([wave_z[1]] * (NP // 128), axis=1)
    for octant in range(8):
        sx, sy, sz = 1 - 2 * (octant % 2), 1 - 2 * (octant // 2 % 2), 1 - 2 * (octant // 4)
        xy = times((x_real, sx * x_imag), (y_real, sy * y_imag))
        full = times(xy, (z_real, sz * z_imag))
        phase[octant, 0], phase[octant, 1] = full

    pl.semaphore_wait(barrier, MEM - 1 + jnp.minimum(group, 1) + jnp.minimum(groups - 1 - group, 1))

    width = BAND // HALO_PARTS

    def up(n, to):
        return pltpu.make_async_remote_copy(
            src_ref=patterns.at[pl.ds(CL - BAND + n * width, width)],
            dst_ref=wide.at[pl.ds(n * width, width)],
            send_sem=halo_send.at[0, n],
            recv_sem=halo_recv.at[0, n],
            device_id=(to, me),
            device_id_type=MESH,
        )

    def down(n, to):
        return pltpu.make_async_remote_copy(
            src_ref=patterns.at[pl.ds(n * width, width)],
            dst_ref=wide.at[pl.ds(CL + BAND + n * width, width)],
            send_sem=halo_send.at[1, n],
            recv_sem=halo_recv.at[1, n],
            device_id=(to, me),
            device_id_type=MESH,
        )

    def start_halo():
        for n in range(HALO_PARTS):

            @pl.when(has_above)
            def _():
                up(n, above).start()

            @pl.when(has_below)
            def _():
                down(n, below).start()

    @pl.when(core == 0)
    def _():
        start_halo()

    def translate(cluster, cells, first):
        real = jnp.zeros((LAT, NP), jnp.float32)
        imag = jnp.zeros((LAT, NP), jnp.float32)
        for p in range(NPART):
            cell = cells[jnp.clip(partners[p, cluster] - first, 0, cells.shape[0] - 1)]
            factor = ops[factors[p, cluster]]
            part = times(factor, cell)
            real, imag = real + part[0], imag + part[1]
        translated[cluster, 0] = real
        translated[cluster, 1] = imag

    for one in loads[2:6]:
        one.wait()

    @pl.loop(BAND, CL - BAND)
    def _(cluster):
        translate(cluster, own, group * CL)

    def wait_sent():
        for n in range(HALO_PARTS):

            @pl.when(has_above)
            def _():
                up(n, above).wait_send()

            @pl.when(has_below)
            def _():
                down(n, below).wait_send()

    for one in loads[6:10]:
        one.wait()
    inner = []
    for child in range(CH):
        row = lax.rem(parents[child], CL)
        inner.append(jnp.where((row >= BAND) & (row < CL - BAND), 1, 0))
    count = sum(inner)
    seen = jnp.int32(0)
    lane = lax.broadcasted_iota(jnp.int32, (8, 128), 1)
    child_of = jnp.zeros((8, 128), jnp.int32)
    for child in range(CH):
        place = jnp.where(inner[child] == 1, seen, count + child - seen)
        rank[child] = place
        child_of = jnp.where(lane == place, child, child_of)
        seen = seen + inner[child]
    order_held[...] = child_of
    ordering = pltpu.make_async_copy(order_held, order, load_sem.at[0])
    ordering.start()
    ordering.wait()

    def shift_and_reduce(begin, end, first, number):
        rounds = end - begin
        for n in range(number):
            for k in range(rounds):
                child = order[0, (begin + k) * FIRST + chips[first + n] // 2]
                parent = translated[lax.rem(parents[child], CL)]
                moved = times(parent, phase[octants[child]])
                h, l = halves(jnp.concatenate(moved, axis=0))
                at = (n * rounds + k) * 2 * LAT
                high[at : at + 2 * LAT, :] = h
                low[at : at + 2 * LAT, :] = l
        total = number * rounds * 2 * LAT
        h, l = high[:total, :], low[:total, :]
        result = dot(h, phi_high[...]) + dot(h, phi_low[...]) + dot(l, phi_high[...])
        result = result.reshape(number, rounds, 2, LAT, NPC)
        for n in range(number):
            made[begin:end, first + n] = result[n]

    def send(index, chip, part):
        begin, end = ROUNDS[index]
        pltpu.make_async_remote_copy(
            src_ref=made.at[pl.ds(begin, end - begin), chip, part],
            dst_ref=got.at[pl.ds(begin, end - begin), me],
            send_sem=send_sem.at[index],
            recv_sem=recv_sem.at[index],
            device_id=(group, chips[chip] + part),
            device_id_type=MESH,
        ).start()

    def send_chips(index, first, number):
        begin, end = ROUNDS[index]
        for chip in range(first, first + number):
            if chip < CHIPS - 1:
                send(index, chip, 0)
                send(index, chip, 1)
            else:
                send(index, chip, 1 - core)
                got[begin:end, me] = made[begin:end, chip, core]

    def wait_for(blocks, sem):
        pltpu.make_async_copy(blocks, blocks, sem).wait()

    for first in range(0, CHIPS, PART):
        shift_and_reduce(*ROUNDS[0], first, PART)

    send_chips(0, 0, CHIPS)

    @pl.when(core == 0)
    def _():
        wait_sent()
        pl.semaphore_signal(turn, inc=1, device_id=(group, chips[-1] + 1), device_id_type=MESH)

    @pl.when(core == 1)
    def _():
        pl.semaphore_wait(turn, 1)
        start_halo()

    for one in loads[10:]:
        one.wait()

    def mine(index):
        begin, end = ROUNDS[index]
        return pltpu.make_async_copy(
            thin.at[pl.ds(begin, end - begin), me],
            out.at[pl.ds(begin, end - begin), me // 2, core],
            load_sem.at[1 + index],
        )

    def finish(index):
        begin, end = ROUNDS[index]
        rounds = pl.ds(begin, end - begin)
        wait_for(got.at[rounds, pl.ds(0, MEM - 1)], recv_sem.at[index])
        for k in range(begin, end):
            h, l = halves(got[k].reshape(NT, NPC))
            result = dot(theta_high[...], h) + dot(theta_low[...], h) + dot(theta_high[...], l)
            thin[k] = result.reshape(MEM, OUT_LAT, NPC)
        for member in others:
            pltpu.make_async_remote_copy(
                src_ref=thin.at[rounds, member],
                dst_ref=out.at[rounds, me // 2, core],
                send_sem=back_send.at[index],
                recv_sem=back_recv.at[index],
                device_id=(group, member),
                device_id_type=MESH,
            ).start()
        mine(index).start()

    @pl.when(core == 1)
    def _():
        finish(0)

    for n in range(HALO_PARTS):

        @pl.when(has_above)
        def _():
            down(n, above).wait_recv()

        @pl.when(has_below)
        def _():
            up(n, below).wait_recv()

    @pl.loop(0, 2 * BAND)
    def _(n):
        translate(jnp.where(n < BAND, n, n + CL - 2 * BAND), wide, group * CL - BAND)

    for index in range(1, len(ROUNDS)):
        begin, end = ROUNDS[index]
        number = PART // (end - begin)
        for first in range(0, CHIPS, number):
            shift_and_reduce(begin, end, first, number)
            send_chips(index, first, number)
    @pl.when(core == 0)
    def _():
        finish(0)

    for index in range(1, len(ROUNDS)):
        finish(index)

    @pl.when(core == 1)
    def _():
        wait_sent()

    for index, (begin, end) in enumerate(ROUNDS):
        rounds = pl.ds(begin, end - begin)
        mine(index).wait()
        wait_for(got.at[rounds, pl.ds(0, MEM - 1)], send_sem.at[index])
        wait_for(thin.at[rounds, pl.ds(0, MEM - 1)], back_send.at[index])
        wait_for(thin.at[rounds, pl.ds(0, MEM - 1)], back_recv.at[index])


def reorder(rank_in, ranked, out, rank, ordered, load_sem, store_sem):
    ranks = pltpu.make_async_copy(rank_in, rank, load_sem)
    ranks.start()
    parts = 4
    number = CH // parts

    def store(part):
        rows = pl.ds(part * number, number)
        return pltpu.make_async_copy(ordered.at[rows], out.at[rows], store_sem.at[part])

    ranks.wait()
    for part in range(parts):
        for child in range(part * number, (part + 1) * number):
            ordered[child] = ranked[rank[child]]
        store(part).start()
    for part in range(parts):
        store(part).wait()


def on_device(patterns, operators, partners, operator_index, child_parent, child_octant, *, constants):
    f32, bf16 = jnp.float32, jnp.bfloat16
    hbm = pl.BlockSpec(memory_space=pltpu.HBM)
    dma = pltpu.SemaphoreType.DMA
    operands = (partners.T, operator_index.T, child_parent, child_octant, patterns, operators, *constants)
    ranked, rank = pl.pallas_call(
        kernel,
        out_shape=(
            pltpu.VMEM((CH // FIRST, CHIPS, 2, OUT_LAT, NPC), f32),
            jax.ShapeDtypeStruct((CH,), jnp.int32),
        ),
        in_specs=[hbm] * (6 + len(constants)),
        out_specs=(pl.BlockSpec(memory_space=pltpu.VMEM), pl.BlockSpec(memory_space=pltpu.SMEM)),
        scratch_shapes=[
            pltpu.SMEM((NPART, CL), jnp.int32),
            pltpu.SMEM((NPART, CL), jnp.int32),
            pltpu.SMEM((CH,), jnp.int32),
            pltpu.SMEM((CH,), jnp.int32),
            pltpu.VMEM((CL, 2, LAT, NP), f32),
            pltpu.VMEM((CL + 2 * BAND, 2, LAT, NP), f32),
            pltpu.VMEM(operators.shape, f32),
            pltpu.VMEM((2, LAT, NP), f32),
            pltpu.VMEM((2, LAT, 128), f32),
            pltpu.VMEM((NP, NPC), bf16),
            pltpu.VMEM((NP, NPC), bf16),
            pltpu.VMEM((NTC, NT), bf16),
            pltpu.VMEM((NTC, NT), bf16),
            pltpu.SMEM((8, 128), jnp.int32),
            pltpu.VMEM((8, 128), jnp.int32),
            pltpu.VMEM((8, 2, LAT, NP), f32),
            pltpu.VMEM((CL, 2, LAT, NP), f32),
            pltpu.VMEM((PART * 2 * LAT, NP), bf16),
            pltpu.VMEM((PART * 2 * LAT, NP), bf16),
            pltpu.VMEM((CH // FIRST, CHIPS, 2, LAT, NPC), f32),
            pltpu.VMEM((CH // FIRST, MEM, LAT, NPC), f32),
            pltpu.VMEM((CH // FIRST, MEM, OUT_LAT, NPC), f32),
            dma((13,)),
            dma((2, HALO_PARTS)),
            dma((2, HALO_PARTS)),
            dma((len(ROUNDS),)),
            dma((len(ROUNDS),)),
            dma((len(ROUNDS),)),
            dma((len(ROUNDS),)),
            pltpu.SemaphoreType.REGULAR,
        ],
        compiler_params=pltpu.CompilerParams(
            collective_id=0, has_side_effects=True, vmem_limit_bytes=40 * 2**20
        ),
        cost_estimate=pl.CostEstimate(flops=10**9, bytes_accessed=6 * 2**20, transcendentals=0),
    )(*(pltpu.with_memory_space_constraint(jnp.asarray(x), pltpu.HBM) for x in operands))
    shape = (CH, 2, OUT_LAT, NPC)
    return pl.pallas_call(
        reorder,
        out_shape=jax.ShapeDtypeStruct(shape, f32),
        in_specs=[hbm, pl.BlockSpec(memory_space=pltpu.VMEM)],
        out_specs=hbm,
        scratch_shapes=[pltpu.SMEM((CH,), jnp.int32), pltpu.VMEM(shape, f32), dma(()), dma((4,))],
        compiler_params=pltpu.CompilerParams(vmem_limit_bytes=40 * 2**20),
    )(rank, ranked.reshape(shape))


def solution(mesh):
    constants = tables()
    whole = P("group", None, "member", None)
    return jax.shard_map(
        functools.partial(on_device, constants=constants),
        mesh=mesh,
        in_specs=(whole, P(None, None, "member", None), P("group", None), P("group", None), P("group"), P("group")),
        out_specs=whole,
        check_vma=False,
    )
```

```python
import functools

import jax
import jax.numpy as jnp
import ml_dtypes
import numpy as np
from jax import lax
from jax.experimental import pallas as pl
from jax.experimental.pallas import tpu as pltpu
from jax.sharding import PartitionSpec as P

MESH = pl.DeviceIdType.MESH

NT, NP, NTC, NPC = 256, 512, 128, 256
NPART = 8
CL = 32
CH = 64
BAND = 8
MEM = 32
LAT = NT // MEM
OUT_LAT = NTC // MEM
REACH = 6.0
HALO_PARTS = 1
FIRST = 16
CHIPS = 16
ROUNDS = ((0, 1), (1, 2), (2, 3), (3, 4))
PART = 8
STEPS = sorted(
    ((y, x) for y in range(4) for x in range(4)),
    key=lambda step: -min(step[0], 4 - step[0]) - min(step[1], 4 - step[1]),
)


def split(values):
    high = values.astype(ml_dtypes.bfloat16)
    low = (values - high.astype(np.float64)).astype(ml_dtypes.bfloat16)
    return high, low


def tables():
    theta_fine = np.pi * (np.arange(NT) + 0.5) / NT
    theta_coarse = np.pi * (np.arange(NTC) + 0.5) / NTC
    orders = np.arange(NTC)
    weights = np.where(orders > 0, 2.0, 1.0)
    theta = (np.cos(np.outer(theta_coarse, orders)) * weights) @ np.cos(np.outer(theta_fine, orders)).T / NT
    phi_fine = 2.0 * np.pi * np.arange(NP) / NP
    phi_coarse = 2.0 * np.pi * np.arange(NPC) / NPC
    modes = np.arange(NPC // 2 + 1)
    mode_weights = np.where((modes > 0) & (modes < NPC // 2), 2.0, 1.0)
    phi = (
        (np.cos(np.outer(phi_coarse, modes)) * mode_weights) @ np.cos(np.outer(phi_fine, modes)).T
        + (np.sin(np.outer(phi_coarse, modes)) * mode_weights) @ np.sin(np.outer(phi_fine, modes)).T
    ) / NP
    theta_high, theta_low = split(theta)
    phi_high, phi_low = split(phi.T)
    arg = REACH * np.sin(theta_fine)[:, None] * np.cos(phi_fine)[None, :]
    wave_x = np.stack([np.cos(arg), np.sin(arg)]).reshape(2, MEM, LAT, NP).swapaxes(0, 1)
    arg = np.broadcast_to(REACH * np.cos(theta_fine)[:, None], (NT, 128))
    wave_z = np.stack([np.cos(arg), np.sin(arg)]).reshape(2, MEM, LAT, 128).swapaxes(0, 1)
    return (
        wave_x.astype(np.float32),
        wave_z.astype(np.float32),
        phi_high,
        phi_low,
        theta_high,
        theta_low,
    )


def times(a, b):
    return a[0] * b[0] - a[1] * b[1], a[0] * b[1] + a[1] * b[0]


def halves(x):
    high = x.astype(jnp.bfloat16)
    return high, (x - high.astype(jnp.float32)).astype(jnp.bfloat16)


def dot(a, b):
    return jnp.dot(a, b, preferred_element_type=jnp.float32)


def kernel(
    partners_in, factors_in, parents_in, octants_in, patterns, operators, wave_x_in, wave_z_in, phi_high_in, phi_low_in, theta_high_in, theta_low_in,
    out, rank,
    partners, factors, parents, octants,
    own, wide, ops, wave_x, wave_z, phi_high, phi_low, theta_high, theta_low,
    order, order_held, phase, translated, high, low, made, got, thin,
    load_sem, halo_send, halo_recv, send_sem, recv_sem, back_send, back_recv, turn,
):
    group = lax.axis_index("group")
    me = lax.axis_index("member")
    groups = lax.axis_size("group")
    below, above = group - 1, group + 1
    has_below, has_above = group > 0, group < groups - 1

    def load(k, src, dst):
        return pltpu.make_async_copy(src, dst, load_sem.at[k])

    loads = [
        load(0, wave_x_in.at[me], wave_x),
        load(1, wave_z_in.at[me], wave_z),
        load(2, partners_in, partners),
        load(3, factors_in, factors),
        load(4, patterns, own),
        load(5, operators, ops),
        load(6, parents_in, parents),
        load(7, octants_in, octants),
        load(8, phi_high_in, phi_high),
        load(9, phi_low_in, phi_low),
        load(10, patterns, wide.at[pl.ds(BAND, CL)]),
        load(11, theta_high_in, theta_high),
        load(12, theta_low_in, theta_low),
    ]
    for one in loads:
        one.start()

    core = lax.rem(me, 2)
    late = lax.rem(me + me // 8 + me // 2, 2)
    ys = [lax.rem(me // 8 + step, 4) * 8 for step in range(4)]
    xs = [lax.rem(me // 2 + step, 4) * 2 for step in range(4)]
    chips = [ys[y] + xs[x] for y, x in STEPS]
    others = [chip + part for chip in chips[:-1] for part in range(2)] + [chips[-1] + 1 - core]

    barrier = pltpu.get_barrier_semaphore()

    @pl.when(has_above)
    def _():
        pl.semaphore_signal(barrier, inc=1, device_id=(above, me), device_id_type=MESH)

    @pl.when(has_below)
    def _():
        pl.semaphore_signal(barrier, inc=1, device_id=(below, me), device_id_type=MESH)

    for member in others:
        pl.semaphore_signal(barrier, inc=1, device_id=(group, member), device_id_type=MESH)

    for one in loads[:2]:
        one.wait()
    x_real, x_imag = wave_x[0], wave_x[1]

    def turned(v):
        return jnp.concatenate([v[:, NP - NP // 4 :], v[:, : NP - NP // 4]], axis=1)

    y_real, y_imag = turned(x_real), turned(x_imag)
    z_real = jnp.concatenate([wave_z[0]] * (NP // 128), axis=1)
    z_imag = jnp.concatenate([wave_z[1]] * (NP // 128), axis=1)
    for octant in range(8):
        sx, sy, sz = 1 - 2 * (octant % 2), 1 - 2 * (octant // 2 % 2), 1 - 2 * (octant // 4)
        xy = times((x_real, sx * x_imag), (y_real, sy * y_imag))
        full = times(xy, (z_real, sz * z_imag))
        phase[octant, 0], phase[octant, 1] = full

    pl.semaphore_wait(barrier, MEM - 1 + jnp.minimum(group, 1) + jnp.minimum(groups - 1 - group, 1))

    width = BAND // HALO_PARTS

    def up(n, to):
        return pltpu.make_async_remote_copy(
            src_ref=patterns.at[pl.ds(CL - BAND + n * width, width)],
            dst_ref=wide.at[pl.ds(n * width, width)],
            send_sem=halo_send.at[0, n],
            recv_sem=halo_recv.at[0, n],
            device_id=(to, me),
            device_id_type=MESH,
        )

    def down(n, to):
        return pltpu.make_async_remote_copy(
            src_ref=patterns.at[pl.ds(n * width, width)],
            dst_ref=wide.at[pl.ds(CL + BAND + n * width, width)],
            send_sem=halo_send.at[1, n],
            recv_sem=halo_recv.at[1, n],
            device_id=(to, me),
            device_id_type=MESH,
        )

    def start_halo():
        for n in range(HALO_PARTS):

            @pl.when(has_above)
            def _():
                up(n, above).start()

            @pl.when(has_below)
            def _():
                down(n, below).start()

    @pl.when(late == 0)
    def _():
        start_halo()

    def translate(cluster, cells, first):
        real = jnp.zeros((LAT, NP), jnp.float32)
        imag = jnp.zeros((LAT, NP), jnp.float32)
        for p in range(NPART):
            cell = cells[jnp.clip(partners[p, cluster] - first, 0, cells.shape[0] - 1)]
            factor = ops[factors[p, cluster]]
            part = times(factor, cell)
            real, imag = real + part[0], imag + part[1]
        translated[cluster, 0] = real
        translated[cluster, 1] = imag

    for one in loads[2:6]:
        one.wait()

    @pl.loop(BAND, CL - BAND)
    def _(cluster):
        translate(cluster, own, group * CL)

    def wait_sent():
        for n in range(HALO_PARTS):

            @pl.when(has_above)
            def _():
                up(n, above).wait_send()

            @pl.when(has_below)
            def _():
                down(n, below).wait_send()

    for one in loads[6:10]:
        one.wait()
    inner = []
    for child in range(CH):
        row = lax.rem(parents[child], CL)
        inner.append(jnp.where((row >= BAND) & (row < CL - BAND), 1, 0))
    count = sum(inner)
    seen = jnp.int32(0)
    lane = lax.broadcasted_iota(jnp.int32, (8, 128), 1)
    child_of = jnp.zeros((8, 128), jnp.int32)
    for child in range(CH):
        place = jnp.where(inner[child] == 1, seen, count + child - seen)
        rank[child] = place
        child_of = jnp.where(lane == place, child, child_of)
        seen = seen + inner[child]
    order_held[...] = child_of
    ordering = pltpu.make_async_copy(order_held, order, load_sem.at[0])
    ordering.start()
    ordering.wait()

    def shift_and_reduce(begin, end, first, number):
        rounds = end - begin
        for n in range(number):
            for k in range(rounds):
                child = order[0, (begin + k) * FIRST + chips[first + n] // 2]
                parent = translated[lax.rem(parents[child], CL)]
                moved = times(parent, phase[octants[child]])
                h, l = halves(jnp.concatenate(moved, axis=0))
                at = (n * rounds + k) * 2 * LAT
                high[at : at + 2 * LAT, :] = h
                low[at : at + 2 * LAT, :] = l
        total = number * rounds * 2 * LAT
        h, l = high[:total, :], low[:total, :]
        result = dot(h, phi_high[...]) + dot(h, phi_low[...]) + dot(l, phi_high[...])
        result = result.reshape(number, rounds, 2, LAT, NPC)
        for n in range(number):
            made[begin:end, first + n] = result[n]

    def send(index, chip, part):
        begin, end = ROUNDS[index]
        pltpu.make_async_remote_copy(
            src_ref=made.at[pl.ds(begin, end - begin), chip, part],
            dst_ref=got.at[pl.ds(begin, end - begin), me],
            send_sem=send_sem.at[index],
            recv_sem=recv_sem.at[index],
            device_id=(group, chips[chip] + part),
            device_id_type=MESH,
        ).start()

    def send_chips(index, first, number):
        begin, end = ROUNDS[index]
        for chip in range(first, first + number):
            if chip < CHIPS - 1:
                send(index, chip, 0)
                send(index, chip, 1)
            else:
                send(index, chip, 1 - core)
                got[begin:end, me] = made[begin:end, chip, core]

    def wait_for(blocks, sem):
        pltpu.make_async_copy(blocks, blocks, sem).wait()

    for first in range(0, CHIPS, PART):
        shift_and_reduce(*ROUNDS[0], first, PART)

    send_chips(0, 0, CHIPS)

    @pl.when(late == 0)
    def _():
        wait_sent()
        pl.semaphore_signal(turn, inc=1, device_id=(group, chips[-1] + 1 - core), device_id_type=MESH)

    @pl.when(late == 1)
    def _():
        pl.semaphore_wait(turn, 1)
        start_halo()

    for one in loads[10:]:
        one.wait()

    def mine(index):
        begin, end = ROUNDS[index]
        return pltpu.make_async_copy(
            thin.at[pl.ds(begin, end - begin), me],
            out.at[pl.ds(begin, end - begin), me // 2, core],
            load_sem.at[1 + index],
        )

    def finish(index):
        begin, end = ROUNDS[index]
        rounds = pl.ds(begin, end - begin)
        wait_for(got.at[rounds, pl.ds(0, MEM - 1)], recv_sem.at[index])
        for k in range(begin, end):
            h, l = halves(got[k].reshape(NT, NPC))
            result = dot(theta_high[...], h) + dot(theta_low[...], h) + dot(theta_high[...], l)
            thin[k] = result.reshape(MEM, OUT_LAT, NPC)
        for member in others:
            pltpu.make_async_remote_copy(
                src_ref=thin.at[rounds, member],
                dst_ref=out.at[rounds, me // 2, core],
                send_sem=back_send.at[index],
                recv_sem=back_recv.at[index],
                device_id=(group, member),
                device_id_type=MESH,
            ).start()
        mine(index).start()

    @pl.when(late == 1)
    def _():
        finish(0)

    for n in range(HALO_PARTS):

        @pl.when(has_above)
        def _():
            down(n, above).wait_recv()

        @pl.when(has_below)
        def _():
            up(n, below).wait_recv()

    @pl.loop(0, 2 * BAND)
    def _(n):
        translate(jnp.where(n < BAND, n, n + CL - 2 * BAND), wide, group * CL - BAND)

    for index in range(1, len(ROUNDS)):
        begin, end = ROUNDS[index]
        number = PART // (end - begin)
        for first in range(0, CHIPS, number):
            shift_and_reduce(begin, end, first, number)
            send_chips(index, first, number)
    @pl.when(late == 0)
    def _():
        finish(0)

    for index in range(1, len(ROUNDS)):
        finish(index)

    @pl.when(late == 1)
    def _():
        wait_sent()

    for index, (begin, end) in enumerate(ROUNDS):
        rounds = pl.ds(begin, end - begin)
        mine(index).wait()
        wait_for(got.at[rounds, pl.ds(0, MEM - 1)], send_sem.at[index])
        wait_for(thin.at[rounds, pl.ds(0, MEM - 1)], back_send.at[index])
        wait_for(thin.at[rounds, pl.ds(0, MEM - 1)], back_recv.at[index])


def reorder(rank_in, ranked, out, rank, ordered, load_sem, store_sem):
    ranks = pltpu.make_async_copy(rank_in, rank, load_sem)
    ranks.start()
    parts = 4
    number = CH // parts

    def store(part):
        rows = pl.ds(part * number, number)
        return pltpu.make_async_copy(ordered.at[rows], out.at[rows], store_sem.at[part])

    ranks.wait()
    for part in range(parts):
        for child in range(part * number, (part + 1) * number):
            ordered[child] = ranked[rank[child]]
        store(part).start()
    for part in range(parts):
        store(part).wait()


def on_device(patterns, operators, partners, operator_index, child_parent, child_octant, *, constants):
    f32, bf16 = jnp.float32, jnp.bfloat16
    hbm = pl.BlockSpec(memory_space=pltpu.HBM)
    dma = pltpu.SemaphoreType.DMA
    operands = (partners.T, operator_index.T, child_parent, child_octant, patterns, operators, *constants)
    ranked, rank = pl.pallas_call(
        kernel,
        out_shape=(
            pltpu.VMEM((CH // FIRST, CHIPS, 2, OUT_LAT, NPC), f32),
            jax.ShapeDtypeStruct((CH,), jnp.int32),
        ),
        in_specs=[hbm] * (6 + len(constants)),
        out_specs=(pl.BlockSpec(memory_space=pltpu.VMEM), pl.BlockSpec(memory_space=pltpu.SMEM)),
        scratch_shapes=[
            pltpu.SMEM((NPART, CL), jnp.int32),
            pltpu.SMEM((NPART, CL), jnp.int32),
            pltpu.SMEM((CH,), jnp.int32),
            pltpu.SMEM((CH,), jnp.int32),
            pltpu.VMEM((CL, 2, LAT, NP), f32),
            pltpu.VMEM((CL + 2 * BAND, 2, LAT, NP), f32),
            pltpu.VMEM(operators.shape, f32),
            pltpu.VMEM((2, LAT, NP), f32),
            pltpu.VMEM((2, LAT, 128), f32),
            pltpu.VMEM((NP, NPC), bf16),
            pltpu.VMEM((NP, NPC), bf16),
            pltpu.VMEM((NTC, NT), bf16),
            pltpu.VMEM((NTC, NT), bf16),
            pltpu.SMEM((8, 128), jnp.int32),
            pltpu.VMEM((8, 128), jnp.int32),
            pltpu.VMEM((8, 2, LAT, NP), f32),
            pltpu.VMEM((CL, 2, LAT, NP), f32),
            pltpu.VMEM((PART * 2 * LAT, NP), bf16),
            pltpu.VMEM((PART * 2 * LAT, NP), bf16),
            pltpu.VMEM((CH // FIRST, CHIPS, 2, LAT, NPC), f32),
            pltpu.VMEM((CH // FIRST, MEM, LAT, NPC), f32),
            pltpu.VMEM((CH // FIRST, MEM, OUT_LAT, NPC), f32),
            dma((13,)),
            dma((2, HALO_PARTS)),
            dma((2, HALO_PARTS)),
            dma((len(ROUNDS),)),
            dma((len(ROUNDS),)),
            dma((len(ROUNDS),)),
            dma((len(ROUNDS),)),
            pltpu.SemaphoreType.REGULAR,
        ],
        compiler_params=pltpu.CompilerParams(
            collective_id=0, has_side_effects=True, vmem_limit_bytes=40 * 2**20
        ),
        cost_estimate=pl.CostEstimate(flops=10**9, bytes_accessed=6 * 2**20, transcendentals=0),
    )(*(pltpu.with_memory_space_constraint(jnp.asarray(x), pltpu.HBM) for x in operands))
    shape = (CH, 2, OUT_LAT, NPC)
    return pl.pallas_call(
        reorder,
        out_shape=jax.ShapeDtypeStruct(shape, f32),
        in_specs=[hbm, pl.BlockSpec(memory_space=pltpu.VMEM)],
        out_specs=hbm,
        scratch_shapes=[pltpu.SMEM((CH,), jnp.int32), pltpu.VMEM(shape, f32), dma(()), dma((4,))],
        compiler_params=pltpu.CompilerParams(vmem_limit_bytes=40 * 2**20),
    )(rank, ranked.reshape(shape))


def solution(mesh):
    constants = tables()
    whole = P("group", None, "member", None)
    return jax.shard_map(
        functools.partial(on_device, constants=constants),
        mesh=mesh,
        in_specs=(whole, P(None, None, "member", None), P("group", None), P("group", None), P("group"), P("group")),
        out_specs=whole,
        check_vma=False,
    )
```

```python
import functools

import jax
import jax.numpy as jnp
import ml_dtypes
import numpy as np
from jax import lax
from jax.experimental import pallas as pl
from jax.experimental.pallas import tpu as pltpu
from jax.sharding import PartitionSpec as P

MESH = pl.DeviceIdType.MESH

NT, NP, NTC, NPC = 256, 512, 128, 256
NPART = 8
CL = 32
CH = 64
BAND = 8
MEM = 32
LAT = NT // MEM
OUT_LAT = NTC // MEM
REACH = 6.0
HALO_PARTS = 1
FIRST = 16
CHIPS = 16
ROUNDS = ((0, 1), (1, 2), (2, 3), (3, 4))
PART = 8
STEPS = sorted(
    ((y, x) for y in range(4) for x in range(4)),
    key=lambda step: -min(step[0], 4 - step[0]) - min(step[1], 4 - step[1]),
)


def split(values):
    high = values.astype(ml_dtypes.bfloat16)
    low = (values - high.astype(np.float64)).astype(ml_dtypes.bfloat16)
    return high, low


def tables():
    theta_fine = np.pi * (np.arange(NT) + 0.5) / NT
    theta_coarse = np.pi * (np.arange(NTC) + 0.5) / NTC
    orders = np.arange(NTC)
    weights = np.where(orders > 0, 2.0, 1.0)
    theta = (np.cos(np.outer(theta_coarse, orders)) * weights) @ np.cos(np.outer(theta_fine, orders)).T / NT
    phi_fine = 2.0 * np.pi * np.arange(NP) / NP
    phi_coarse = 2.0 * np.pi * np.arange(NPC) / NPC
    modes = np.arange(NPC // 2 + 1)
    mode_weights = np.where((modes > 0) & (modes < NPC // 2), 2.0, 1.0)
    phi = (
        (np.cos(np.outer(phi_coarse, modes)) * mode_weights) @ np.cos(np.outer(phi_fine, modes)).T
        + (np.sin(np.outer(phi_coarse, modes)) * mode_weights) @ np.sin(np.outer(phi_fine, modes)).T
    ) / NP
    theta_high, theta_low = split(theta)
    phi_high, phi_low = split(phi.T)
    arg = REACH * np.sin(theta_fine)[:, None] * np.cos(phi_fine)[None, :]
    wave_x = np.stack([np.cos(arg), np.sin(arg)]).reshape(2, MEM, LAT, NP).swapaxes(0, 1)
    arg = np.broadcast_to(REACH * np.cos(theta_fine)[:, None], (NT, 128))
    wave_z = np.stack([np.cos(arg), np.sin(arg)]).reshape(2, MEM, LAT, 128).swapaxes(0, 1)
    return (
        wave_x.astype(np.float32),
        wave_z.astype(np.float32),
        phi_high,
        phi_low,
        theta_high,
        theta_low,
    )


def times(a, b):
    return a[0] * b[0] - a[1] * b[1], a[0] * b[1] + a[1] * b[0]


def halves(x):
    high = x.astype(jnp.bfloat16)
    return high, (x - high.astype(jnp.float32)).astype(jnp.bfloat16)


def dot(a, b):
    return jnp.dot(a, b, preferred_element_type=jnp.float32)


def kernel(
    partners_in, factors_in, parents_in, octants_in, patterns, operators, wave_x_in, wave_z_in, phi_high_in, phi_low_in, theta_high_in, theta_low_in,
    out, rank,
    partners, factors, parents, octants,
    own, wide, ops, wave_x, wave_z, phi_high, phi_low, theta_high, theta_low,
    order, order_held, phase, translated, high, low, made, got, thin,
    load_sem, halo_send, halo_recv, send_sem, recv_sem, back_send, back_recv, turn,
):
    group = lax.axis_index("group")
    me = lax.axis_index("member")
    groups = lax.axis_size("group")
    below, above = group - 1, group + 1
    has_below, has_above = group > 0, group < groups - 1

    def load(k, src, dst):
        return pltpu.make_async_copy(src, dst, load_sem.at[k])

    loads = [
        load(0, wave_x_in.at[me], wave_x),
        load(1, wave_z_in.at[me], wave_z),
        load(2, partners_in, partners),
        load(3, factors_in, factors),
        load(4, patterns, own),
        load(5, operators, ops),
        load(6, parents_in, parents),
        load(7, octants_in, octants),
        load(8, phi_high_in, phi_high),
        load(9, phi_low_in, phi_low),
        load(10, patterns, wide.at[pl.ds(BAND, CL)]),
        load(11, theta_high_in, theta_high),
        load(12, theta_low_in, theta_low),
    ]
    for one in loads:
        one.start()

    core = lax.rem(me, 2)
    ys = [lax.rem(me // 8 + step, 4) * 8 for step in range(4)]
    xs = [lax.rem(me // 2 + step, 4) * 2 for step in range(4)]
    chips = [ys[y] + xs[x] for y, x in STEPS]
    others = [chip + part for chip in chips[:-1] for part in range(2)] + [chips[-1] + 1 - core]

    barrier = pltpu.get_barrier_semaphore()

    @pl.when(has_above)
    def _():
        pl.semaphore_signal(barrier, inc=1, device_id=(above, me), device_id_type=MESH)

    @pl.when(has_below)
    def _():
        pl.semaphore_signal(barrier, inc=1, device_id=(below, me), device_id_type=MESH)

    for member in others:
        pl.semaphore_signal(barrier, inc=1, device_id=(group, member), device_id_type=MESH)

    for one in loads[:2]:
        one.wait()
    x_real, x_imag = wave_x[0], wave_x[1]

    def turned(v):
        return jnp.concatenate([v[:, NP - NP // 4 :], v[:, : NP - NP // 4]], axis=1)

    y_real, y_imag = turned(x_real), turned(x_imag)
    z_real = jnp.concatenate([wave_z[0]] * (NP // 128), axis=1)
    z_imag = jnp.concatenate([wave_z[1]] * (NP // 128), axis=1)
    for octant in range(8):
        sx, sy, sz = 1 - 2 * (octant % 2), 1 - 2 * (octant // 2 % 2), 1 - 2 * (octant // 4)
        xy = times((x_real, sx * x_imag), (y_real, sy * y_imag))
        full = times(xy, (z_real, sz * z_imag))
        phase[octant, 0], phase[octant, 1] = full

    pl.semaphore_wait(barrier, MEM - 1 + jnp.minimum(group, 1) + jnp.minimum(groups - 1 - group, 1))

    width = BAND // HALO_PARTS

    def up(n, to):
        return pltpu.make_async_remote_copy(
            src_ref=patterns.at[pl.ds(CL - BAND + n * width, width)],
            dst_ref=wide.at[pl.ds(n * width, width)],
            send_sem=halo_send.at[0, n],
            recv_sem=halo_recv.at[0, n],
            device_id=(to, me),
            device_id_type=MESH,
        )

    def down(n, to):
        return pltpu.make_async_remote_copy(
            src_ref=patterns.at[pl.ds(n * width, width)],
            dst_ref=wide.at[pl.ds(CL + BAND + n * width, width)],
            send_sem=halo_send.at[1, n],
            recv_sem=halo_recv.at[1, n],
            device_id=(to, me),
            device_id_type=MESH,
        )

    def start_halo():
        for n in range(HALO_PARTS):

            @pl.when(has_above)
            def _():
                up(n, above).start()

            @pl.when(has_below)
            def _():
                down(n, below).start()

    @pl.when(core == 0)
    def _():
        start_halo()

    def translate(cluster, cells, first):
        real = jnp.zeros((LAT, NP), jnp.float32)
        imag = jnp.zeros((LAT, NP), jnp.float32)
        for p in range(NPART):
            cell = cells[jnp.clip(partners[p, cluster] - first, 0, cells.shape[0] - 1)]
            factor = ops[factors[p, cluster]]
            part = times(factor, cell)
            real, imag = real + part[0], imag + part[1]
        translated[cluster, 0] = real
        translated[cluster, 1] = imag

    for one in loads[2:6]:
        one.wait()

    @pl.loop(BAND, CL - BAND)
    def _(cluster):
        translate(cluster, own, group * CL)

    def wait_sent():
        for n in range(HALO_PARTS):

            @pl.when(has_above)
            def _():
                up(n, above).wait_send()

            @pl.when(has_below)
            def _():
                down(n, below).wait_send()

    for one in loads[6:10]:
        one.wait()
    inner = []
    for child in range(CH):
        row = lax.rem(parents[child], CL)
        inner.append(jnp.where((row >= BAND) & (row < CL - BAND), 1, 0))
    count = sum(inner)
    seen = jnp.int32(0)
    lane = lax.broadcasted_iota(jnp.int32, (8, 128), 1)
    child_of = jnp.zeros((8, 128), jnp.int32)
    for child in range(CH):
        place = jnp.where(inner[child] == 1, seen, count + child - seen)
        rank[child] = place
        child_of = jnp.where(lane == place, child, child_of)
        seen = seen + inner[child]
    order_held[...] = child_of
    ordering = pltpu.make_async_copy(order_held, order, load_sem.at[0])
    ordering.start()
    ordering.wait()

    def shift_and_reduce(begin, end, first, number):
        rounds = end - begin
        for n in range(number):
            for k in range(rounds):
                child = order[0, (begin + k) * FIRST + chips[first + n] // 2]
                parent = translated[lax.rem(parents[child], CL)]
                moved = times(parent, phase[octants[child]])
                h, l = halves(jnp.concatenate(moved, axis=0))
                at = (n * rounds + k) * 2 * LAT
                high[at : at + 2 * LAT, :] = h
                low[at : at + 2 * LAT, :] = l
        total = number * rounds * 2 * LAT
        h, l = high[:total, :], low[:total, :]
        result = dot(h, phi_high[...]) + dot(h, phi_low[...]) + dot(l, phi_high[...])
        result = result.reshape(number, rounds, 2, LAT, NPC)
        for n in range(number):
            made[begin:end, first + n] = result[n]

    def send(index, chip, part):
        begin, end = ROUNDS[index]
        pltpu.make_async_remote_copy(
            src_ref=made.at[pl.ds(begin, end - begin), chip, part],
            dst_ref=got.at[pl.ds(begin, end - begin), me],
            send_sem=send_sem.at[index],
            recv_sem=recv_sem.at[index],
            device_id=(group, chips[chip] + part),
            device_id_type=MESH,
        ).start()

    def send_chips(index, first, number):
        begin, end = ROUNDS[index]
        for chip in range(first, first + number):
            if chip < CHIPS - 1:
                send(index, chip, 0)
                send(index, chip, 1)
            else:
                send(index, chip, 1 - core)
                got[begin:end, me] = made[begin:end, chip, core]

    def wait_for(blocks, sem):
        pltpu.make_async_copy(blocks, blocks, sem).wait()

    for first in range(0, CHIPS, PART):
        shift_and_reduce(*ROUNDS[0], first, PART)

    send_chips(0, 0, CHIPS)

    @pl.when(core == 0)
    def _():
        wait_sent()
        pl.semaphore_signal(turn, inc=1, device_id=(group, chips[-1] + 1), device_id_type=MESH)

    @pl.when(core == 1)
    def _():
        pl.semaphore_wait(turn, 1)
        start_halo()

    for one in loads[10:]:
        one.wait()

    def mine(index):
        begin, end = ROUNDS[index]
        return pltpu.make_async_copy(
            thin.at[pl.ds(begin, end - begin), me],
            out.at[pl.ds(begin, end - begin), me // 2, core],
            load_sem.at[1 + index],
        )

    def finish(index):
        begin, end = ROUNDS[index]
        rounds = pl.ds(begin, end - begin)
        wait_for(got.at[rounds, pl.ds(0, MEM - 1)], recv_sem.at[index])
        for k in range(begin, end):
            h, l = halves(got[k].reshape(NT, NPC))
            result = dot(theta_high[...], h) + dot(theta_low[...], h) + dot(theta_high[...], l)
            thin[k] = result.reshape(MEM, OUT_LAT, NPC)
        for member in others:
            pltpu.make_async_remote_copy(
                src_ref=thin.at[rounds, member],
                dst_ref=out.at[rounds, me // 2, core],
                send_sem=back_send.at[index],
                recv_sem=back_recv.at[index],
                device_id=(group, member),
                device_id_type=MESH,
            ).start()
        mine(index).start()

    @pl.when(core == 1)
    def _():
        finish(0)

    for n in range(HALO_PARTS):

        @pl.when(has_above)
        def _():
            down(n, above).wait_recv()

        @pl.when(has_below)
        def _():
            up(n, below).wait_recv()

    @pl.loop(0, 2 * BAND)
    def _(n):
        translate(jnp.where(n < BAND, n, n + CL - 2 * BAND), wide, group * CL - BAND)

    for index in range(1, len(ROUNDS)):
        begin, end = ROUNDS[index]
        number = PART // (end - begin)
        for first in range(0, CHIPS, number):
            shift_and_reduce(begin, end, first, number)
            send_chips(index, first, number)
        if index == 2:

            @pl.when(core == 0)
            def _():
                finish(0)

    for index in range(1, len(ROUNDS)):
        finish(index)

    @pl.when(core == 1)
    def _():
        wait_sent()

    for index, (begin, end) in enumerate(ROUNDS):
        rounds = pl.ds(begin, end - begin)
        mine(index).wait()
        wait_for(got.at[rounds, pl.ds(0, MEM - 1)], send_sem.at[index])
        wait_for(thin.at[rounds, pl.ds(0, MEM - 1)], back_send.at[index])
        wait_for(thin.at[rounds, pl.ds(0, MEM - 1)], back_recv.at[index])


def reorder(rank_in, ranked, out, rank, ordered, load_sem, store_sem):
    ranks = pltpu.make_async_copy(rank_in, rank, load_sem)
    ranks.start()
    parts = 4
    number = CH // parts

    def store(part):
        rows = pl.ds(part * number, number)
        return pltpu.make_async_copy(ordered.at[rows], out.at[rows], store_sem.at[part])

    ranks.wait()
    for part in range(parts):
        for child in range(part * number, (part + 1) * number):
            ordered[child] = ranked[rank[child]]
        store(part).start()
    for part in range(parts):
        store(part).wait()


def on_device(patterns, operators, partners, operator_index, child_parent, child_octant, *, constants):
    f32, bf16 = jnp.float32, jnp.bfloat16
    hbm = pl.BlockSpec(memory_space=pltpu.HBM)
    dma = pltpu.SemaphoreType.DMA
    operands = (partners.T, operator_index.T, child_parent, child_octant, patterns, operators, *constants)
    ranked, rank = pl.pallas_call(
        kernel,
        out_shape=(
            pltpu.VMEM((CH // FIRST, CHIPS, 2, OUT_LAT, NPC), f32),
            jax.ShapeDtypeStruct((CH,), jnp.int32),
        ),
        in_specs=[hbm] * (6 + len(constants)),
        out_specs=(pl.BlockSpec(memory_space=pltpu.VMEM), pl.BlockSpec(memory_space=pltpu.SMEM)),
        scratch_shapes=[
            pltpu.SMEM((NPART, CL), jnp.int32),
            pltpu.SMEM((NPART, CL), jnp.int32),
            pltpu.SMEM((CH,), jnp.int32),
            pltpu.SMEM((CH,), jnp.int32),
            pltpu.VMEM((CL, 2, LAT, NP), f32),
            pltpu.VMEM((CL + 2 * BAND, 2, LAT, NP), f32),
            pltpu.VMEM(operators.shape, f32),
            pltpu.VMEM((2, LAT, NP), f32),
            pltpu.VMEM((2, LAT, 128), f32),
            pltpu.VMEM((NP, NPC), bf16),
            pltpu.VMEM((NP, NPC), bf16),
            pltpu.VMEM((NTC, NT), bf16),
            pltpu.VMEM((NTC, NT), bf16),
            pltpu.SMEM((8, 128), jnp.int32),
            pltpu.VMEM((8, 128), jnp.int32),
            pltpu.VMEM((8, 2, LAT, NP), f32),
            pltpu.VMEM((CL, 2, LAT, NP), f32),
            pltpu.VMEM((PART * 2 * LAT, NP), bf16),
            pltpu.VMEM((PART * 2 * LAT, NP), bf16),
            pltpu.VMEM((CH // FIRST, CHIPS, 2, LAT, NPC), f32),
            pltpu.VMEM((CH // FIRST, MEM, LAT, NPC), f32),
            pltpu.VMEM((CH // FIRST, MEM, OUT_LAT, NPC), f32),
            dma((13,)),
            dma((2, HALO_PARTS)),
            dma((2, HALO_PARTS)),
            dma((len(ROUNDS),)),
            dma((len(ROUNDS),)),
            dma((len(ROUNDS),)),
            dma((len(ROUNDS),)),
            pltpu.SemaphoreType.REGULAR,
        ],
        compiler_params=pltpu.CompilerParams(
            collective_id=0, has_side_effects=True, vmem_limit_bytes=40 * 2**20
        ),
        cost_estimate=pl.CostEstimate(flops=10**9, bytes_accessed=6 * 2**20, transcendentals=0),
    )(*(pltpu.with_memory_space_constraint(jnp.asarray(x), pltpu.HBM) for x in operands))
    shape = (CH, 2, OUT_LAT, NPC)
    return pl.pallas_call(
        reorder,
        out_shape=jax.ShapeDtypeStruct(shape, f32),
        in_specs=[hbm, pl.BlockSpec(memory_space=pltpu.VMEM)],
        out_specs=hbm,
        scratch_shapes=[pltpu.SMEM((CH,), jnp.int32), pltpu.VMEM(shape, f32), dma(()), dma((4,))],
        compiler_params=pltpu.CompilerParams(vmem_limit_bytes=40 * 2**20),
    )(rank, ranked.reshape(shape))


def solution(mesh):
    constants = tables()
    whole = P("group", None, "member", None)
    return jax.shard_map(
        functools.partial(on_device, constants=constants),
        mesh=mesh,
        in_specs=(whole, P(None, None, "member", None), P("group", None), P("group", None), P("group"), P("group")),
        out_specs=whole,
        check_vma=False,
    )
```
